32 devices in a mesh: span: 4 (over z), grp: 8 (over y, x, core).
Axes of the slice: x: 2, y: 2, z: 4, core: 2. Of those that a mesh axis runs over, the one named last changes fastest.
Arguments:
- displacement: float32 [4, 5, 8192], P('span', None, 'grp'), may hold values from -3 to 3
- velocity: float32 [4, 5, 8192], P('span', None, 'grp'), may hold values from -3 to 3
- nodal_load: float32 [4, 5, 8192], P('span', None, 'grp'), may hold values from -6 to 6
- nodal_mass: float32 [4, 8192], P('span', 'grp'), may hold values from 1 to 4
- plastic_strain: float32 [4, 128, 3, 5, 128], P('span', 'grp'), may hold values from -0.3 to 0.3
- hardening: float32 [4, 128, 5, 128], P('span', 'grp'), may hold values from 0 to 0.2
- ply_modulus: float32 [4, 128, 5, 128], P('span', 'grp'), may hold values from 0.5 to 2
- inverse_size: float32 [4, 128, 128], P('span', 'grp'), may hold values from 0.5 to 2
- cost_map: int32 [4, 128], P('span'), may hold values from 1 to 4
- migration_plan: int32 [4, 128, 1], P('span'), may hold values from 0 to 7; in each aligned block of 16 rows (0 to 15, 16 to 31, ..., all dimensions but the last counted through in order) at most 2 rows name the same one
- block_nodes: int32 [4, 128, 256], P('span'), may hold values from 0 to 8383, as said below
- corner_slot: int32 [4, 128, 4, 128], P('span'), may hold values from 0 to 255
Outputs:
- displacement_out: float32 [4, 5, 8192], P('span', None, 'grp')
- velocity_out: float32 [4, 5, 8192], P('span', None, 'grp')
- resident_plastic: float32 [4, 128, 3, 5, 128], P('span', 'grp')
- resident_hardening: float32 [4, 128, 5, 128], P('span', 'grp')
The draws below stay inside these ranges and needn't reach their ends.
Inputs may be any that keep to these rules, and one draw needn't show every extreme that they name: `migration_plan`: of the 16 blocks that start on one device (aligned blocks of 16 entries), no more than 2 name the same device. `cost_map`: newton turns of a block. `block_nodes`: block b of a span group (0 to 127) lists 256 distinct nodes from b * (64) on.
All inputs are finite; a program needn't handle non-finite values.
Results may differ from the reference program's by a relative error of at most 0.0003.
Values sent between devices are 32-bit elements; how exact they have to be, the bound alone decides.
A program may use at most 64 MiB of HBM per device.

```python
import math
import jax
import jax.numpy as jnp
import numpy as np
from jax import lax

NOWN = 1024
BLK = 16
EL = 128
PTS = 5
WINDOW = 256
NEWTON = 4
STEPS = 4
CAP = 2
NGN = 8192
N_SPAN = 4
N_GRP = 8


def draw_block_nodes(key, part):
    count = N_SPAN * N_GRP * BLK
    keys = jax.random.split(jax.random.fold_in(key, 7), count)

    def one_list(subkey):
        return jax.random.permutation(subkey, WINDOW)
    lists = jax.vmap(one_list)(keys).astype(jnp.int32).reshape(N_SPAN, N_GRP * BLK, WINDOW)
    base = jnp.arange(N_GRP * BLK, dtype=jnp.int32) * (NOWN // BLK)
    return (base[None, :, None] + lists).astype(jnp.int32)


def with_ends(drawn, key, low, high):
    shape = drawn.shape
    spot = [jax.random.randint(jax.random.fold_in(key, axis), (), 0, shape[axis]) for axis in range(len(shape))]
    drawn = drawn.at[tuple(spot)].set(low)
    longest = shape.index(max(shape))
    spot[longest] = (spot[longest] + 1) % shape[longest]
    return drawn.at[tuple(spot)].set(high)


def block_scale(rng, dims, cuts, least, high):
    level = 1.0
    for axis_at, blocks in cuts:
        steps = jax.random.uniform(jax.random.fold_in(jax.random.fold_in(rng, 6), axis_at), (blocks,), jnp.float32, least / len(cuts), high / len(cuts))
        level = level * jnp.repeat(jnp.exp(steps), dims[axis_at] // blocks).reshape((-1,) + (1,) * (len(dims) - 1 - axis_at))
    return level


def shared_out(own_key, own, number, rows, count, top, reach, lean):
    ranking = jax.random.permutation(own_key, count)
    crowded, ordinary = load_shares(count, rows * top, reach, lean, True), load_shares(count, rows * top, reach, lean, False)
    places = jnp.arange(count)

    def named(sizes, offset_by):
        used = int((sizes > 0).sum())
        fixed = max(1, used // 4)
        passed = fixed + (places - fixed + offset_by * (used - fixed)) % max(1, count - fixed)
        return jnp.zeros((count,), jnp.int32).at[ranking[jnp.where(places < fixed, places, passed)]].set(jnp.asarray(sizes, jnp.int32))

    sizes = jnp.where(number % 4 == 0, named(crowded, number // 4), named(ordinary, number - number // 4 - 1))
    mixed = jax.random.permutation(jax.random.fold_in(own, 3), count)
    donor, sink = mixed[0:count // 2 * 2:2], mixed[1:count // 2 * 2:2]
    margin = jnp.minimum(sizes[donor] - 1, reach - sizes[sink]) // 2
    margin = jnp.where((donor == ranking[0]) | (sink == ranking[0]) | (sizes[sink] == 0), 0, jnp.maximum(margin, 0))
    passed = jax.random.randint(jax.random.fold_in(own, 4), (count // 2,), 0, 1 << 20) % (margin + 1)
    sizes = sizes.at[donor].add(-passed).at[sink].add(passed)
    members = jnp.searchsorted(jnp.cumsum(sizes), jnp.arange(rows * top), side="right").astype(jnp.int32)
    table = members.reshape(top, rows).T
    table = table[jax.random.permutation(jax.random.fold_in(own, 1), rows)]
    offset_by = jax.random.randint(jax.random.fold_in(own, 2), (rows, 1), 0, top)
    return jnp.take_along_axis(table, (jnp.arange(top)[None, :] + offset_by) % top, axis=1)


def load_shares(number_of, total, limit, slope, full):
    weights = [(1 << 20) // math.isqrt(grade ** slope) + 1 for grade in range(1, number_of + 1)]
    largest = limit if full else min(limit, max(-(-total // number_of), total * weights[0] // sum(weights)))
    least = 1 if total - largest >= number_of - 1 else 0
    holding, surplus = [largest] + [least] * (number_of - 1), total - largest - least * (number_of - 1)
    while surplus > 0:
        free = [i for i in range(1, number_of) if holding[i] < largest] or [i for i in range(1, number_of) if holding[i] < limit]
        pool, remaining = sum([weights[i] for i in free]), surplus
        for i in free:
            extra = min(limit - holding[i], max(1, remaining * weights[i] // pool), surplus)
            holding[i] = holding[i] + extra
            surplus = surplus - extra
    return np.array(holding)


def centred(rng, dims, width, most, shards=(), held_as=jnp.bfloat16):
    values = jax.random.normal(rng, dims, jnp.float32) * width
    if len(shards) > 0:
        values = block_scale(rng, dims, shards, -0.22, 0.18) * values
    return jnp.clip(values, min=-most, max=most).astype(held_as)


def setup_inputs(seed: int = 0) -> dict:
    seeds = jax.random.split(jax.random.key(seed), 13)
    displacement = centred(seeds[0], (N_SPAN, 5, NGN), 0.5, 3.0, ((0, 4), (2, 8)), jnp.float32)
    velocity = centred(seeds[1], (N_SPAN, 5, NGN), 0.5, 3.0, ((0, 4), (2, 8)), jnp.float32)
    nodal_load = centred(seeds[2], (N_SPAN, 5, NGN), 1.0, 6.0, ((0, 4), (2, 8)), jnp.float32)
    nodal_mass = jnp.clip(jnp.exp(math.log(4.0) - 1.3862944 * jax.random.uniform(seeds[3], (N_SPAN, NGN), jnp.float32) ** block_scale(seeds[3], (N_SPAN, NGN), ((0, 4), (1, 8)), -0.2, 0.2)), 1.0, 4.0)
    plastic_strain = centred(seeds[4], (N_SPAN, N_GRP * BLK, 3, PTS, EL), 0.05, 0.3, ((0, 4), (1, 8)), jnp.float32)
    hardening = jnp.clip(0.2 * jax.random.uniform(seeds[5], (N_SPAN, N_GRP * BLK, PTS, EL), jnp.float32) ** block_scale(seeds[5], (N_SPAN, N_GRP * BLK, PTS, EL), ((0, 4), (1, 8)), -0.2, 0.2), 0.0, 0.2)
    ply_modulus = jnp.clip(jnp.exp(math.log(2.0) - 1.3862944 * jax.random.uniform(seeds[6], (N_SPAN, N_GRP * BLK, PTS, EL), jnp.float32) ** block_scale(seeds[6], (N_SPAN, N_GRP * BLK, PTS, EL), ((0, 4), (1, 8)), -0.2, 0.2)), 0.5, 2.0)
    inverse_size = jnp.clip(jnp.exp(math.log(2.0) - 1.3862944 * jax.random.uniform(seeds[7], (N_SPAN, N_GRP * BLK, EL), jnp.float32) ** block_scale(seeds[7], (N_SPAN, N_GRP * BLK, EL), ((0, 4), (1, 8)), -0.2, 0.2)), 0.5, 2.0)
    cost_map = with_ends(jax.random.randint(seeds[8], (N_SPAN, N_GRP * BLK), 1, NEWTON + 1), jax.random.fold_in(seeds[8], 1), 1, NEWTON).astype(jnp.int32)
    migration_plan_keys = jax.random.split(jax.random.fold_in(seeds[9], 1), N_SPAN * (N_GRP * BLK) // BLK)
    migration_plan_turns = jax.random.permutation(jax.random.fold_in(seeds[9], 3), N_SPAN * (N_GRP * BLK) // BLK)
    migration_plan = jax.vmap(lambda own, number: shared_out(jax.random.fold_in(seeds[9], 2), own, number, BLK, N_GRP, 1, CAP, 1))(migration_plan_keys, migration_plan_turns).reshape((N_SPAN, N_GRP * BLK, 1))
    block_nodes = draw_block_nodes(jax.random.fold_in(seeds[12], 71), 0)
    corner_slot = with_ends(jax.random.randint(seeds[11], (N_SPAN, N_GRP * BLK, 4, EL), 0, WINDOW), jax.random.fold_in(seeds[11], 1), 0, WINDOW - 1).astype(jnp.int32)
    return dict(displacement=displacement, velocity=velocity, nodal_load=nodal_load, nodal_mass=nodal_mass, plastic_strain=plastic_strain, hardening=hardening, ply_modulus=ply_modulus, inverse_size=inverse_size, cost_map=cost_map, migration_plan=migration_plan, block_nodes=block_nodes, corner_slot=corner_slot)


POISSON = 0.3
YIELD = 0.1
SATURATE = 0.1
RATE = 20.0
STEP_TIME = 0.25

def element_update(corner_disp, inverse_size, modulus, plastic, harden, costs):
    corner_a = corner_disp[:, :, 0]
    corner_b = corner_disp[:, :, 1]
    corner_c = corner_disp[:, :, 2]
    corner_d = corner_disp[:, :, 3]
    inverse = inverse_size[:, None, :]
    deriv_x = 0.5 * inverse * (corner_b + corner_c - corner_a - corner_d)
    deriv_y = 0.5 * inverse * (corner_c + corner_d - corner_a - corner_b)
    centre = 0.25 * (corner_a + corner_b + corner_c + corner_d)
    membrane = jnp.stack([deriv_x[:, 0], deriv_y[:, 1], deriv_y[:, 0] + deriv_x[:, 1]], 1)
    bending = jnp.stack([deriv_x[:, 3], deriv_y[:, 4], deriv_y[:, 3] + deriv_x[:, 4]], 1)
    transverse = jnp.stack([deriv_x[:, 2] + centre[:, 3], deriv_y[:, 2] + centre[:, 4]], 1)
    heights = jnp.array([-0.5, -0.25, 0.0, 0.25, 0.5], jnp.float32)
    through = jnp.array([1.0, 4.0, 2.0, 4.0, 1.0], jnp.float32) / 12.0
    strains = membrane[:, :, None, :] + heights[None, None, :, None] * bending[:, :, None, :]
    elastic = strains - plastic
    stiffness = modulus / (1.0 - POISSON * POISSON)
    trial_stress = jnp.stack([stiffness * (elastic[:, 0] + POISSON * elastic[:, 1]), stiffness * (POISSON * elastic[:, 0] + elastic[:, 1]), stiffness * 0.5 * (1.0 - POISSON) * elastic[:, 2]], 1)
    equivalent = jnp.sqrt((trial_stress[:, 0] - 0.5 * trial_stress[:, 1]) ** 2 + 0.75 * trial_stress[:, 1] ** 2 + 3.0 * trial_stress[:, 2] ** 2)
    shear_three = 1.5 * modulus / (1.0 + POISSON)
    initial_yield = YIELD + SATURATE * (1.0 - jnp.exp(-RATE * harden))
    step_size = jnp.zeros_like(equivalent)
    for newton_turn in range(NEWTON):
        hardness = harden + step_size
        decay_term = jnp.exp(-RATE * hardness)
        mismatch = equivalent - shear_three * step_size - YIELD - SATURATE * (1.0 - decay_term)
        tangent = shear_three + SATURATE * RATE * decay_term
        active = (newton_turn < costs)[:, None, None]
        step_size = jnp.where(active, step_size + mismatch / tangent, step_size)
    step_size = jnp.where(equivalent > initial_yield, step_size, 0.0)
    shrink = 1.0 - shear_three * step_size / jnp.maximum(equivalent, YIELD)
    stresses = shrink[:, None] * trial_stress
    plastic_new = plastic + (1.0 - shrink)[:, None] * elastic
    harden_new = harden + step_size
    membrane_force = lax.optimization_barrier(jnp.sum(through[None, None, :, None] * stresses, axis=2))
    moments = lax.optimization_barrier(jnp.sum((through * heights)[None, None, :, None] * stresses, axis=2))
    shear_modulus = 5.0 / 6.0 * lax.optimization_barrier(jnp.sum(through[None, :, None] * modulus, axis=1)) / (2.0 * (1.0 + POISSON))
    shear_force = shear_modulus[:, None, :] * transverse
    weight_x = jnp.array([-0.5, 0.5, 0.5, -0.5], jnp.float32)[None, :, None]
    weight_y = jnp.array([-0.5, -0.5, 0.5, 0.5], jnp.float32)[None, :, None]
    force_u = inverse * (weight_x * membrane_force[:, 0:1] + weight_y * membrane_force[:, 2:3])
    force_v = inverse * (weight_y * membrane_force[:, 1:2] + weight_x * membrane_force[:, 2:3])
    force_w = inverse * (weight_x * shear_force[:, 0:1] + weight_y * shear_force[:, 1:2])
    force_a = inverse * (weight_x * moments[:, 0:1] + weight_y * moments[:, 2:3]) + 0.25 * shear_force[:, 0:1]
    force_b = inverse * (weight_y * moments[:, 1:2] + weight_x * moments[:, 2:3]) + 0.25 * shear_force[:, 1:2]
    forces = jnp.stack([force_u, force_v, force_w, force_a, force_b], 1)
    return (forces, plastic_new, harden_new)

def reference(displacement, velocity, nodal_load, nodal_mass, plastic_strain, hardening, ply_modulus, inverse_size, cost_map, migration_plan, block_nodes, corner_slot):
    spans = displacement.shape[0]
    group_nodes = displacement.shape[2]
    blocks = plastic_strain.shape[1]
    points = plastic_strain.shape[3]
    elements = plastic_strain.shape[4]
    window = block_nodes.shape[2]
    extended_nodes = group_nodes + window
    corner_node = jnp.take_along_axis(block_nodes, corner_slot.reshape(spans, blocks, 4 * elements).astype(jnp.int32), axis=2)
    span_index = jnp.arange(spans, dtype=jnp.int32)
    flat_index = (span_index[:, None, None] * extended_nodes + corner_node).reshape(-1).astype(jnp.int32)
    plastic = plastic_strain.reshape(spans * blocks, 3, points, elements)
    harden = hardening.reshape(spans * blocks, points, elements)
    modulus = ply_modulus.reshape(spans * blocks, points, elements)
    inverse = inverse_size.reshape(spans * blocks, elements)
    costs = cost_map.reshape(-1)
    root = (span_index[:, None, None] == 0) & (jnp.arange(group_nodes)[None, None, :] < window)
    disp_now = displacement
    vel_now = velocity
    for time_step in range(STEPS):
        beyond = jnp.concatenate([disp_now[1:, :, :window], jnp.zeros((1, 5, window), jnp.float32)], 0)
        extended = jnp.concatenate([disp_now, beyond], 2)
        table = jnp.transpose(extended, (0, 2, 1)).reshape(spans * extended_nodes, 5)
        corner_disp = table[flat_index].reshape(spans * blocks, 4, elements, 5)
        corner_disp = jnp.transpose(corner_disp, (0, 3, 1, 2))
        forces, plastic, harden = element_update(corner_disp, inverse, modulus, plastic, harden, costs)
        corner_forces = jnp.transpose(forces, (0, 2, 3, 1)).reshape(-1, 5)
        assembled = jax.ops.segment_sum(corner_forces, flat_index, num_segments=spans * extended_nodes)
        assembled = jnp.transpose(assembled.reshape(spans, extended_nodes, 5), (0, 2, 1))
        carried = jnp.concatenate([jnp.zeros((1, 5, window), jnp.float32), assembled[:-1, :, group_nodes:]], 0)
        carried = jnp.pad(carried, ((0, 0), (0, 0), (0, group_nodes - window)))
        internal = assembled[:, :, :group_nodes] + carried
        accel = (nodal_load - internal) / nodal_mass[:, None, :]
        vel_now = jnp.where(root, 0.0, vel_now + STEP_TIME * accel)
        disp_now = disp_now + STEP_TIME * vel_now
    per_device = blocks // N_GRP
    dests = migration_plan[:, :, 0].reshape(spans, N_GRP, per_device)
    earlier = jnp.arange(per_device)[:, None] > jnp.arange(per_device)[None, :]
    same = dests[:, :, :, None] == dests[:, :, None, :]
    rank = lax.optimization_barrier(jnp.sum(same & earlier[None, None], axis=3)).astype(jnp.int32)
    target = (dests * (N_GRP * CAP) + jnp.arange(N_GRP, dtype=jnp.int32)[None, :, None] * CAP + rank).astype(jnp.int32)
    rows = span_index[:, None, None]
    out_plastic = jnp.zeros((spans, N_GRP * N_GRP * CAP, 3, points, elements), jnp.float32)
    out_plastic = out_plastic.at[rows, target].set(plastic.reshape(spans, N_GRP, per_device, 3, points, elements))
    out_harden = jnp.zeros((spans, N_GRP * N_GRP * CAP, points, elements), jnp.float32)
    out_harden = out_harden.at[rows, target].set(harden.reshape(spans, N_GRP, per_device, points, elements))
    return (disp_now, vel_now, out_plastic, out_harden)
```

```python
import functools

import jax
import jax.numpy as jnp
from jax import lax
from jax.experimental import pallas as pl
from jax.experimental.pallas import tpu as pltpu
from jax.sharding import PartitionSpec as P

NEWTON = 4
STEPS = 4

POISSON = 0.3
YIELD = 0.1
SATURATE = 0.1
RATE = 20.0
STEP_TIME = 0.25
HEIGHTS = (-0.5, -0.25, 0.0, 0.25, 0.5)
THROUGH = (1.0 / 12.0, 4.0 / 12.0, 2.0 / 12.0, 4.0 / 12.0, 1.0 / 12.0)
WEIGHT_X = (-0.5, 0.5, 0.5, -0.5)
WEIGHT_Y = (-0.5, -0.5, 0.5, 0.5)
MESH = pl.DeviceIdType.MESH
LANES = 128
ROWS = 8
FREE = 5


def pad_rows(x):
    return jnp.concatenate([x, jnp.zeros((ROWS - x.shape[0], x.shape[1]), x.dtype)], 0)


def lane_take(x, index):
    return jnp.take_along_axis(x, index, axis=1, mode="promise_in_bounds")


def split_rows(ref_rows, reach):
    return (
        jnp.concatenate([ref_rows[:reach], ref_rows[-reach:]], 0),
        ref_rows[reach:-reach],
    )


def join_rows(outer, inner, reach):
    return jnp.concatenate([outer[:reach], inner, outer[reach:]], 0)


def kernel(
    sizes,
    disp_hbm, vel_hbm, load_hbm, mass_hbm, plastic_hbm, harden_hbm, modulus_hbm, inverse_hbm,
    cost_hbm, plan_hbm, nodes_hbm, slots_hbm,
    disp_out, vel_out, plastic_out, harden_out,
    disp_in, vel_in, load_in, mass_in, plastic_in, harden_in, modulus_in, inverse_in,
    cost_in, plan_in, nodes_in, slots_in,
    rim_out, rim_in, ahead_out, ahead_in, back_out, back_in,
    disp, vel, load, mass, lane_at, half_at, tables, windows, spread, partial,
    plastic, harden, modulus, inverse, costs, pack_out, pack_in,
    in_sems, rim_sems, ahead_sems, back_sems, move_sems,
):
    spans, group, own_nodes, own_blocks, window, stride, reach, capacity = sizes
    points = harden_in.shape[0]
    corners = slots_in.shape[1]
    own_chunks = own_nodes // LANES
    rim_chunks = window // LANES
    chunks = own_chunks + rim_chunks
    station = lax.axis_index("span")
    member = lax.axis_index("grp")
    has_next = jnp.logical_not((station == spans - 1) & (member == group - 1))
    has_prev = jnp.logical_not((station == 0) & (member == 0))
    next_id = (lax.rem(station + (member + 1) // group, spans), lax.rem(member + 1, group))
    prev_id = (
        lax.rem(station + spans - 1 + (member + group - 1) // group, spans),
        lax.rem(member + group - 1, group),
    )
    outer_up = (member == group - 1) & has_next
    outer_down = (member == 0) & has_prev

    barrier = pltpu.get_barrier_semaphore()
    for j in range(1, group):
        pl.semaphore_signal(
            barrier, inc=1, device_id=(station, lax.rem(member + j, group)), device_id_type=MESH
        )

    @pl.when(outer_up)
    def _():
        pl.semaphore_signal(barrier, inc=1, device_id=next_id, device_id_type=MESH)

    @pl.when(outer_down)
    def _():
        pl.semaphore_signal(barrier, inc=1, device_id=prev_id, device_id_type=MESH)

    first = pl.multiple_of(member * own_blocks, own_blocks)
    pairs = [
        (disp_hbm, disp_in),
        (vel_hbm, vel_in),
        (load_hbm, load_in),
        (mass_hbm, mass_in),
        (plastic_hbm, plastic_in),
        (harden_hbm, harden_in),
        (modulus_hbm, modulus_in),
        (inverse_hbm.at[0], inverse_in),
        (cost_hbm, cost_in),
        (plan_hbm, plan_in),
        (nodes_hbm.at[0, pl.ds(first, own_blocks)], nodes_in),
        (slots_hbm.at[0, pl.ds(first, own_blocks)], slots_in),
    ]
    loads = [pltpu.make_async_copy(a, b, in_sems.at[i]) for i, (a, b) in enumerate(pairs)]
    for copy in loads:
        copy.start()
    for copy in loads[:4]:
        copy.wait()
    def cut(q):
        return slice(q * LANES, (q + 1) * LANES)

    def chunk(ref, q):
        return pad_rows(ref[pl.ds(q, FREE, stride=own_chunks), :])

    def mass_chunk(q):
        return jnp.broadcast_to(mass_in[q : q + 1, :], (ROWS, LANES))

    for q in range(rim_chunks):
        for i, ref in enumerate((disp_in, vel_in, load_in)):
            rim_out[i, :, cut(q)] = chunk(ref, q)
        rim_out[3, :, cut(q)] = mass_chunk(q)

    greeted = group - 1 + jnp.where(outer_up, 1, 0) + jnp.where(outer_down, 1, 0)
    pl.semaphore_wait(barrier, greeted)

    def rim_copy():
        return pltpu.make_async_remote_copy(
            src_ref=rim_out, dst_ref=rim_in, send_sem=rim_sems.at[0], recv_sem=rim_sems.at[1],
            device_id=prev_id, device_id_type=MESH,
        )

    def ahead_copy(step):
        return pltpu.make_async_remote_copy(
            src_ref=ahead_out.at[step], dst_ref=ahead_in.at[step],
            send_sem=ahead_sems.at[0, step], recv_sem=ahead_sems.at[1, step],
            device_id=next_id, device_id_type=MESH,
        )

    def back_copy(step):
        return pltpu.make_async_remote_copy(
            src_ref=back_out.at[step], dst_ref=back_in.at[step],
            send_sem=back_sems.at[0, step], recv_sem=back_sems.at[1, step],
            device_id=prev_id, device_id_type=MESH,
        )

    @pl.when(has_prev)
    def _():
        rim_copy().start()

    for q in range(own_chunks):
        for source, target in ((disp_in, disp), (vel_in, vel), (load_in, load)):
            target[:, cut(q)] = chunk(source, q)
        mass[:, cut(q)] = STEP_TIME / mass_chunk(q)
    spread[...] = jnp.zeros_like(spread)
    for copy in loads[8:]:
        copy.wait()
    node_row = lax.broadcasted_iota(jnp.int32, (own_blocks, 1), 0)
    local = nodes_in[...] - (first + node_row) * stride
    halves = window // LANES
    local_groups = split_rows(local, reach)
    for g in range(2):
        for k in range(corners):
            slot = split_rows(slots_in[:, k, :], reach)[g]
            low = slot & (LANES - 1)
            node = lane_take(local_groups[g][:, :LANES], low)
            for h in range(1, halves):
                part = lane_take(local_groups[g][:, h * LANES : (h + 1) * LANES], low)
                node = jnp.where(slot // LANES == h, part, node)
            lane_at[k, g * ROWS : (g + 1) * ROWS, :] = node & (LANES - 1)
            half_at[k, g * ROWS : (g + 1) * ROWS, :] = node // LANES
    lane_row = lax.broadcasted_iota(jnp.int32, (LANES, LANES), 0)

    def build(pos, carry):
        for k in range(corners):
            row = lane_at[k, pl.ds(pos, 1), :]
            hit = jnp.where(lane_row == row, 1.0, 0.0).astype(jnp.bfloat16)
            tables[pos, :, k * LANES : (k + 1) * LANES] = hit
        return carry

    lax.fori_loop(0, own_blocks, build, 0)

    width = cost_in.shape[1]
    at_block = lax.broadcasted_iota(jnp.int32, (own_blocks, width), 1)
    mine = at_block == first + lax.broadcasted_iota(jnp.int32, (own_blocks, width), 0)
    cost_column = jnp.sum(jnp.where(mine, cost_in[...], 0), axis=1, keepdims=True)
    cost_groups = split_rows(cost_column, reach)
    for g in range(2):
        costs[g] = jnp.broadcast_to(cost_groups[g], (ROWS, LANES))
    for copy in loads[4:8]:
        copy.wait()
    inverse_groups = split_rows(inverse_in[...], reach)
    for g in range(2):
        inverse[g] = inverse_groups[g]
    for p in range(points):
        for source, target in ((harden_in, harden), (modulus_in, modulus)):
            parts = split_rows(source[p], reach)
            for g in range(2):
                target[g, p] = parts[g]
        for c in range(3):
            parts = split_rows(plastic_in[c, p], reach)
            for g in range(2):
                plastic[g, c * points + p] = parts[g]

    @pl.when(has_prev)
    def _():
        rim_copy().wait_send()

    @pl.when(has_next)
    def _():
        rim_copy().wait_recv()

    rim = pl.ds(own_nodes, window)
    disp[:, rim] = jnp.where(has_next, rim_in[0], 0.0)
    vel[:, rim] = jnp.where(has_next, rim_in[1], 0.0)
    load[:, rim] = jnp.where(has_next, rim_in[2], 0.0)
    mass[:, rim] = jnp.where(has_next, STEP_TIME / rim_in[3], 0.0)

    order = list(range(reach)) + list(range(own_blocks - reach, own_blocks))
    order += list(range(reach, own_blocks - reach))
    phases = LANES // stride
    lane = lax.broadcasted_iota(jnp.int32, (ROWS, LANES), 1)

    def place_windows():
        shifted = {}
        for r in range(phases):
            for q in range(chunks - (1 if r else 0)):
                value = disp[:, cut(q)]
                if r:
                    left = LANES - r * stride
                    value = jnp.where(
                        lane < left,
                        pltpu.roll(value, left, 1),
                        pltpu.roll(disp[:, cut(q + 1)], left, 1),
                    )
                shifted[r, q] = value
        for pos, block in enumerate(order):
            for h in range(halves):
                value = shifted[block % phases, block // phases + h]
                windows[h, pos * ROWS : (pos + 1) * ROWS, :] = value

    def elements(g):
        lanes_of = [lane_at[k, g * ROWS : (g + 1) * ROWS, :] for k in range(corners)]
        halves_of = [half_at[k, g * ROWS : (g + 1) * ROWS, :] for k in range(corners)]
        corner = []
        for c in range(FREE):
            rows = [windows[h, pl.ds(g * ROWS * ROWS + c, ROWS, stride=ROWS), :] for h in range(halves)]
            values = []
            for k in range(corners):
                value = lane_take(rows[0], lanes_of[k])
                for h in range(1, halves):
                    value = jnp.where(halves_of[k] == h, lane_take(rows[h], lanes_of[k]), value)
                values.append(value)
            corner.append(values)
        z = inverse[g]
        half_z = 0.5 * z
        x = [half_z * (u[1] + u[2] - u[0] - u[3]) for u in corner]
        y = [half_z * (u[2] + u[3] - u[0] - u[1]) for u in corner]
        centre = [0.25 * (u[0] + u[1] + u[2] + u[3]) for u in corner[3:]]
        membrane = (x[0], y[1], y[0] + x[1])
        bending = (x[3], y[4], y[3] + x[4])
        transverse = (x[2] + centre[0], y[2] + centre[1])
        cost = costs[g]
        force = [jnp.zeros_like(z) for _ in range(3)]
        moment = [jnp.zeros_like(z) for _ in range(3)]
        stiff_sum = jnp.zeros_like(z)
        for p in range(points):
            young = modulus[g, p]
            old = harden[g, p]
            e = [membrane[c] + HEIGHTS[p] * bending[c] - plastic[g, c * points + p] for c in range(3)]
            stiff = young * (1.0 / (1.0 - POISSON * POISSON))
            trial = (
                stiff * (e[0] + POISSON * e[1]),
                stiff * (POISSON * e[0] + e[1]),
                stiff * (0.5 * (1.0 - POISSON)) * e[2],
            )
            first_part = trial[0] - 0.5 * trial[1]
            equal = jnp.sqrt(
                first_part * first_part + 0.75 * trial[1] * trial[1] + 3.0 * trial[2] * trial[2]
            )
            three = young * (1.5 / (1.0 + POISSON))
            decay = jnp.exp(-RATE * old)
            gap = equal - (YIELD + SATURATE)
            beyond = gap + SATURATE * decay
            change = beyond / (three + (SATURATE * RATE) * decay)
            yields = beyond > 0.0
            for turn in range(1, NEWTON):
                decay = jnp.exp(-RATE * (old + change))
                miss = gap - three * change + SATURATE * decay
                moved = change + miss / (three + (SATURATE * RATE) * decay)
                change = jnp.where(cost > turn, moved, change)
            change = jnp.where(yields & (cost > 0), change, 0.0)
            drop = three * change / jnp.maximum(equal, YIELD)
            keep = 1.0 - drop
            harden[g, p] = old + change
            for c in range(3):
                plastic[g, c * points + p] += drop * e[c]
                stress = keep * trial[c]
                force[c] = force[c] + THROUGH[p] * stress
                if HEIGHTS[p]:
                    moment[c] = moment[c] + (THROUGH[p] * HEIGHTS[p]) * stress
            stiff_sum = stiff_sum + THROUGH[p] * young
        shear = stiff_sum * (5.0 / 6.0 / (2.0 * (1.0 + POISSON)))
        q = (shear * transverse[0], shear * transverse[1])
        nx, ny, nxy = (z * v for v in force)
        mx, my, mxy = (z * v for v in moment)
        qx, qy = z * q[0], z * q[1]
        for k in range(corners):
            a, b = WEIGHT_X[k], WEIGHT_Y[k]
            values = (
                a * nx + b * nxy,
                b * ny + a * nxy,
                a * qx + b * qy,
                a * mx + b * mxy + 0.25 * q[0],
                b * my + a * mxy + 0.25 * q[1],
            )
            for c in range(FREE):
                for h in range(halves):
                    start = g * ROWS * halves * ROWS + h * ROWS + c
                    spread[k, pl.ds(start, ROWS, stride=halves * ROWS), :] = jnp.where(
                        halves_of[k] == h, values[c], 0.0
                    )

    def assemble(g):
        total = {}
        tall = halves * ROWS
        for pos in range(g * ROWS, (g + 1) * ROWS):
            block = order[pos]
            rows = jnp.concatenate(
                [spread[k, pos * tall : (pos + 1) * tall, :] for k in range(corners)], 1
            )
            high = rows.astype(jnp.bfloat16)
            low = (rows - high.astype(jnp.float32)).astype(jnp.bfloat16)
            out = lax.dot_general(
                jnp.concatenate([high, low], 0), tables[pos], (((1,), (1,)), ((), ())),
                preferred_element_type=jnp.float32,
            )
            out = out[:tall] + out[tall:]
            for h in range(halves):
                key = (block % phases, block // phases + h)
                piece = out[h * ROWS : (h + 1) * ROWS]
                total[key] = total[key] + piece if key in total else piece
        result = {}
        for (r, q), value in total.items():
            if r == 0:
                parts = ((q, value),)
            else:
                left = LANES - r * stride
                turned = pltpu.roll(value, r * stride, 1)
                parts = (
                    (q, jnp.where(lane >= r * stride, turned, 0.0)),
                    (q + 1, jnp.where(lane >= r * stride, 0.0, turned)),
                )
            for at, piece in parts:
                result[at] = result[at] + piece if at in result else piece
        return result

    pinned = (station == 0) & (member == 0)

    def forces(step, last):
        place_windows()
        elements(0)
        sums = assemble(0)
        for i in range(rim_chunks):
            ahead_out[step, :, cut(i)] = sums[own_chunks + i]
            if not last:
                back_out[step, :, cut(i)] = sums[i]

        @pl.when(has_next)
        def _():
            ahead_copy(step).start()

        if not last:
            @pl.when(has_prev)
            def _():
                back_copy(step).start()

        for q in range(chunks):
            partial[:, cut(q)] = sums.get(q, jnp.zeros((ROWS, LANES), jnp.float32))
        elements(1)

    def inner_sums():
        for q, value in assemble(1).items():
            partial[:, cut(q)] += value

    def finish(step, last):
        @pl.when(has_next)
        def _():
            ahead_copy(step).wait_send()

        @pl.when(has_prev)
        def _():
            ahead_copy(step).wait_recv()

        if not last:
            @pl.when(has_prev)
            def _():
                back_copy(step).wait_send()

            @pl.when(has_next)
            def _():
                back_copy(step).wait_recv()

        for q in range(own_chunks if last else chunks):
            internal = partial[:, cut(q)]
            if q < rim_chunks:
                internal = internal + jnp.where(has_prev, ahead_in[step, :, cut(q)], 0.0)
            if q >= own_chunks:
                internal = internal + jnp.where(
                    has_next, back_in[step, :, cut(q - own_chunks)], 0.0
                )
            speed = vel[:, cut(q)] + (load[:, cut(q)] - internal) * mass[:, cut(q)]
            if q < rim_chunks:
                speed = jnp.where(pinned, 0.0, speed)
            place = disp[:, cut(q)] + STEP_TIME * speed
            if last:
                vel_out[pl.ds(q, FREE, stride=own_chunks), :] = speed[:FREE]
                disp_out[pl.ds(q, FREE, stride=own_chunks), :] = place[:FREE]
            else:
                vel[:, cut(q)] = speed
                disp[:, cut(q)] = place

    def one_step(step, carry):
        forces(step, False)
        inner_sums()
        finish(step, False)
        return carry

    lax.fori_loop(0, STEPS - 1, one_step, 0)
    last = STEPS - 1
    forces(last, True)

    plan_column = jnp.sum(jnp.where(mine, plan_in[...], 0), axis=1, keepdims=True)
    row_at = lax.broadcasted_iota(jnp.int32, (own_blocks, own_blocks), 0)
    column_at = lax.broadcasted_iota(jnp.int32, (own_blocks, own_blocks), 1)
    plan_row = jnp.sum(jnp.where(row_at == column_at, plan_column, 0), axis=0, keepdims=True)
    rank = jnp.sum(
        jnp.where((row_at < column_at) & (plan_column == plan_row), 1, 0), axis=0, keepdims=True
    )
    slots_all = group * capacity
    slot_at = lax.broadcasted_iota(jnp.int32, (slots_all, own_blocks), 0)
    pick = jnp.where(slot_at == rank * group + plan_row, 1.0, 0.0)
    pick = jnp.concatenate([pick, pick, pick], 1).astype(jnp.bfloat16)

    def packed(ref, index):
        state = join_rows(ref[0, index], ref[1, index], reach)
        a = state.astype(jnp.bfloat16)
        rest = state - a.astype(jnp.float32)
        b = rest.astype(jnp.bfloat16)
        c = (rest - b.astype(jnp.float32)).astype(jnp.bfloat16)
        return jnp.dot(pick, jnp.concatenate([a, b, c], 0), preferred_element_type=jnp.float32)

    kinds = plastic_in.shape[0]
    fields = (kinds + 1) * points
    tall = fields * capacity
    for f in range(fields):
        rows = packed(plastic, f) if f < kinds * points else packed(harden, f - kinds * points)
        for r in range(capacity):
            pack_out[pl.ds(f * capacity + r, group, stride=tall), :] = rows[r * group : (r + 1) * group]

    def block_of(index):
        return pl.ds(pl.multiple_of(index * tall, ROWS), tall)

    def move(j):
        to = lax.rem(member + j, group)
        return pltpu.make_async_remote_copy(
            src_ref=pack_out.at[block_of(to)], dst_ref=pack_in.at[block_of(member)],
            send_sem=move_sems.at[0, j], recv_sem=move_sems.at[1, j],
            device_id=(station, to), device_id_type=MESH,
        )

    stay = pltpu.make_async_copy(
        pack_out.at[block_of(member)], pack_in.at[block_of(member)], move_sems.at[0, 0]
    )
    for j in range(1, group):
        move(j).start()
    stay.start()
    inner_sums()
    finish(last, True)
    stay.wait()
    for j in range(1, group):
        move(j).wait_send()
        move(j).wait_recv()
    for f in range(fields):
        c, p = f // points, f % points
        target = plastic_out.at[c, p] if c < kinds else harden_out.at[p]
        for r in range(capacity):
            rows = pack_in[pl.ds(f * capacity + r, group, stride=tall), :]
            target[pl.ds(r, group, stride=capacity), :] = rows


def on_device(
    displacement, velocity, nodal_load, nodal_mass, plastic_strain, hardening, ply_modulus,
    inverse_size, cost_map, migration_plan, block_nodes, corner_slot,
):
    spans, group = lax.axis_size("span"), lax.axis_size("grp")
    own_nodes = displacement.shape[2]
    own_blocks, kinds, points, size = plastic_strain.shape[1:]
    window = block_nodes.shape[2]
    corners = corner_slot.shape[2]
    stride = own_nodes // own_blocks
    reach = window // stride
    capacity = max(1, (own_blocks + group - 1) // group)
    halves = window // LANES
    slots_all = group * capacity
    chunks = own_nodes + window
    f32, i32 = jnp.float32, jnp.int32
    sizes = (spans, group, own_nodes, own_blocks, window, stride, reach, capacity)
    vmem = pltpu.VMEM
    dma = pltpu.SemaphoreType.DMA
    every = pl.BlockSpec(memory_space=pltpu.MemorySpace.HBM)
    whole = pl.BlockSpec(memory_space=pltpu.VMEM)
    nodal = (displacement.shape[1] * own_nodes // LANES, LANES)
    masses = (own_nodes // LANES, LANES)
    scratch = [
        vmem(nodal, f32), vmem(nodal, f32), vmem(nodal, f32), vmem(masses, f32),
        vmem((kinds, points, own_blocks, size), f32), vmem((points, own_blocks, size), f32),
        vmem((points, own_blocks, size), f32), vmem(inverse_size.shape[1:], f32),
        vmem(cost_map.shape, i32), vmem(cost_map.shape, i32),
        vmem((own_blocks, window), i32), vmem((own_blocks, corners, size), i32),
        vmem((4, ROWS, window), f32), vmem((4, ROWS, window), f32),
        vmem((STEPS, ROWS, window), f32), vmem((STEPS, ROWS, window), f32),
        vmem((STEPS, ROWS, window), f32), vmem((STEPS, ROWS, window), f32),
        vmem((ROWS, chunks), f32), vmem((ROWS, chunks), f32),
        vmem((ROWS, chunks), f32), vmem((ROWS, chunks), f32),
        vmem((corners, own_blocks, size), i32), vmem((corners, own_blocks, size), i32),
        vmem((own_blocks, LANES, corners * size), jnp.bfloat16),
        vmem((halves, own_blocks * ROWS, LANES), f32),
        vmem((corners, own_blocks * halves * ROWS, size), f32),
        vmem((ROWS, chunks), f32),
        vmem((2, kinds * points, ROWS, size), f32), vmem((2, points, ROWS, size), f32),
        vmem((2, points, ROWS, size), f32), vmem((2, ROWS, size), f32),
        vmem((2, ROWS, size), i32),
        vmem((slots_all * (kinds + 1) * points, size), f32),
        vmem((slots_all * (kinds + 1) * points, size), f32),
        dma((12,)), dma((2,)), dma((2, STEPS)), dma((2, STEPS)), dma((2, group)),
    ]
    disp, vel, moved, hardened = pl.pallas_call(
        functools.partial(kernel, sizes),
        out_shape=(
            jax.ShapeDtypeStruct(nodal, f32),
            jax.ShapeDtypeStruct(nodal, f32),
            jax.ShapeDtypeStruct((kinds, points, slots_all, size), f32),
            jax.ShapeDtypeStruct((points, slots_all, size), f32),
        ),
        in_specs=[every] * 12,
        out_specs=(whole,) * 4,
        scratch_shapes=scratch,
        compiler_params=pltpu.CompilerParams(
            collective_id=0, has_side_effects=True, vmem_limit_bytes=63 * 1024 * 1024
        ),
    )(
        displacement.reshape(nodal), velocity.reshape(nodal), nodal_load.reshape(nodal),
        nodal_mass.reshape(masses), jnp.transpose(plastic_strain[0], (1, 2, 0, 3)),
        jnp.transpose(hardening[0], (1, 0, 2)), jnp.transpose(ply_modulus[0], (1, 0, 2)),
        inverse_size, cost_map, migration_plan.reshape(cost_map.shape), block_nodes, corner_slot,
    )
    return (
        disp.reshape(displacement.shape),
        vel.reshape(displacement.shape),
        jnp.transpose(moved, (2, 0, 1, 3))[None],
        jnp.transpose(hardened, (1, 0, 2))[None],
    )


def solution(mesh):
    return jax.shard_map(
        on_device,
        mesh=mesh,
        in_specs=(
            P("span", None, "grp"),
            P("span", None, "grp"),
            P("span", None, "grp"),
            P("span", "grp"),
            P("span", "grp", None, None, None),
            P("span", "grp", None, None),
            P("span", "grp", None, None),
            P("span", "grp", None),
            P("span", None),
            P("span", None, None),
            P("span", None, None),
            P("span", None, None, None),
        ),
        out_specs=(
            P("span", None, "grp"),
            P("span", None, "grp"),
            P("span", "grp", None, None, None),
            P("span", "grp", None, None),
        ),
        check_vma=False,
    )
```

```python
import functools

import jax
import jax.numpy as jnp
from jax import lax
from jax.experimental import pallas as pl
from jax.experimental.pallas import tpu as pltpu
from jax.sharding import PartitionSpec as P

NEWTON = 4
STEPS = 4

POISSON = 0.3
YIELD = 0.1
SATURATE = 0.1
RATE = 20.0
STEP_TIME = 0.25
HEIGHTS = (-0.5, -0.25, 0.0, 0.25, 0.5)
THROUGH = (1.0 / 12.0, 4.0 / 12.0, 2.0 / 12.0, 4.0 / 12.0, 1.0 / 12.0)
WEIGHT_X = (-0.5, 0.5, 0.5, -0.5)
WEIGHT_Y = (-0.5, -0.5, 0.5, 0.5)
MESH = pl.DeviceIdType.MESH
LANES = 128
ROWS = 8
FREE = 5


def pad_rows(x):
    return jnp.concatenate([x, jnp.zeros((ROWS - x.shape[0], x.shape[1]), x.dtype)], 0)


def lane_take(x, index):
    return jnp.take_along_axis(x, index, axis=1, mode="promise_in_bounds")


def split_rows(ref_rows, reach):
    return (
        jnp.concatenate([ref_rows[:reach], ref_rows[-reach:]], 0),
        ref_rows[reach:-reach],
    )


def join_rows(outer, inner, reach):
    return jnp.concatenate([outer[:reach], inner, outer[reach:]], 0)


def kernel(
    sizes,
    disp_hbm, vel_hbm, load_hbm, mass_hbm, plastic_hbm, harden_hbm, modulus_hbm, inverse_hbm,
    cost_hbm, plan_hbm, nodes_hbm, slots_hbm,
    disp_out, vel_out, plastic_out, harden_out,
    disp_in, vel_in, load_in, mass_in, plastic_in, harden_in, modulus_in, inverse_in,
    cost_in, plan_in, nodes_in, slots_in,
    rim_out, rim_in, ahead_out, ahead_in, back_out, back_in,
    disp, vel, load, mass, lane_at, half_at, tables, windows, spread, partial,
    plastic, harden, modulus, inverse, costs, pack_out, pack_in,
    in_sems, rim_sems, ahead_sems, back_sems, move_sems,
):
    spans, group, own_nodes, own_blocks, window, stride, reach, capacity = sizes
    points = harden_in.shape[0]
    corners = slots_in.shape[1]
    own_chunks = own_nodes // LANES
    rim_chunks = window // LANES
    chunks = own_chunks + rim_chunks
    station = lax.axis_index("span")
    member = lax.axis_index("grp")
    has_next = jnp.logical_not((station == spans - 1) & (member == group - 1))
    has_prev = jnp.logical_not((station == 0) & (member == 0))
    next_id = (lax.rem(station + (member + 1) // group, spans), lax.rem(member + 1, group))
    prev_id = (
        lax.rem(station + spans - 1 + (member + group - 1) // group, spans),
        lax.rem(member + group - 1, group),
    )
    outer_up = (member == group - 1) & has_next
    outer_down = (member == 0) & has_prev

    barrier = pltpu.get_barrier_semaphore()
    for j in range(1, group):
        pl.semaphore_signal(
            barrier, inc=1, device_id=(station, lax.rem(member + j, group)), device_id_type=MESH
        )

    @pl.when(outer_up)
    def _():
        pl.semaphore_signal(barrier, inc=1, device_id=next_id, device_id_type=MESH)

    @pl.when(outer_down)
    def _():
        pl.semaphore_signal(barrier, inc=1, device_id=prev_id, device_id_type=MESH)

    first = pl.multiple_of(member * own_blocks, own_blocks)
    pairs = [
        (disp_hbm, disp_in),
        (vel_hbm, vel_in),
        (load_hbm, load_in),
        (mass_hbm, mass_in),
        (plastic_hbm, plastic_in),
        (harden_hbm, harden_in),
        (modulus_hbm, modulus_in),
        (inverse_hbm.at[0], inverse_in),
        (cost_hbm, cost_in),
        (plan_hbm, plan_in),
        (nodes_hbm.at[0, pl.ds(first, own_blocks)], nodes_in),
        (slots_hbm.at[0, pl.ds(first, own_blocks)], slots_in),
    ]
    loads = [pltpu.make_async_copy(a, b, in_sems.at[i]) for i, (a, b) in enumerate(pairs)]
    for copy in loads:
        copy.start()
    for copy in loads[:4]:
        copy.wait()
    def cut(q):
        return slice(q * LANES, (q + 1) * LANES)

    def chunk(ref, q):
        return pad_rows(ref[pl.ds(q, FREE, stride=own_chunks), :])

    def mass_chunk(q):
        return jnp.broadcast_to(mass_in[q : q + 1, :], (ROWS, LANES))

    for q in range(rim_chunks):
        for i, ref in enumerate((disp_in, vel_in, load_in)):
            rim_out[i, :, cut(q)] = chunk(ref, q)
        rim_out[3, :, cut(q)] = mass_chunk(q)

    greeted = group - 1 + jnp.where(outer_up, 1, 0) + jnp.where(outer_down, 1, 0)
    pl.semaphore_wait(barrier, greeted)

    def rim_copy():
        return pltpu.make_async_remote_copy(
            src_ref=rim_out, dst_ref=rim_in, send_sem=rim_sems.at[0], recv_sem=rim_sems.at[1],
            device_id=prev_id, device_id_type=MESH,
        )

    def ahead_copy(step):
        return pltpu.make_async_remote_copy(
            src_ref=ahead_out.at[step], dst_ref=ahead_in.at[step],
            send_sem=ahead_sems.at[0, step], recv_sem=ahead_sems.at[1, step],
            device_id=next_id, device_id_type=MESH,
        )

    def back_copy(step):
        return pltpu.make_async_remote_copy(
            src_ref=back_out.at[step], dst_ref=back_in.at[step],
            send_sem=back_sems.at[0, step], recv_sem=back_sems.at[1, step],
            device_id=prev_id, device_id_type=MESH,
        )

    @pl.when(has_prev)
    def _():
        rim_copy().start()

    for q in range(own_chunks):
        for source, target in ((disp_in, disp), (vel_in, vel), (load_in, load)):
            target[:, cut(q)] = chunk(source, q)
        mass[:, cut(q)] = STEP_TIME / mass_chunk(q)
    spread[...] = jnp.zeros_like(spread)
    for copy in loads[8:]:
        copy.wait()
    node_row = lax.broadcasted_iota(jnp.int32, (own_blocks, 1), 0)
    local = nodes_in[...] - (first + node_row) * stride
    halves = window // LANES
    local_groups = split_rows(local, reach)
    for g in range(2):
        for k in range(corners):
            slot = split_rows(slots_in[:, k, :], reach)[g]
            low = slot & (LANES - 1)
            node = lane_take(local_groups[g][:, :LANES], low)
            for h in range(1, halves):
                part = lane_take(local_groups[g][:, h * LANES : (h + 1) * LANES], low)
                node = jnp.where(slot // LANES == h, part, node)
            lane_at[k, g * ROWS : (g + 1) * ROWS, :] = node & (LANES - 1)
            half_at[k, g * ROWS : (g + 1) * ROWS, :] = node // LANES
    lane_row = lax.broadcasted_iota(jnp.int32, (LANES, LANES), 0)

    def build(pos, carry):
        for k in range(corners):
            row = lane_at[k, pl.ds(pos, 1), :]
            hit = jnp.where(lane_row == row, 1.0, 0.0).astype(jnp.bfloat16)
            tables[pos, :, k * LANES : (k + 1) * LANES] = hit
        return carry

    lax.fori_loop(0, own_blocks, build, 0)

    width = cost_in.shape[1]
    at_block = lax.broadcasted_iota(jnp.int32, (own_blocks, width), 1)
    mine = at_block == first + lax.broadcasted_iota(jnp.int32, (own_blocks, width), 0)
    cost_column = jnp.sum(jnp.where(mine, cost_in[...], 0), axis=1, keepdims=True)
    cost_groups = split_rows(cost_column, reach)
    for g in range(2):
        costs[g] = jnp.broadcast_to(cost_groups[g], (ROWS, LANES))
    for copy in loads[4:8]:
        copy.wait()
    inverse_groups = split_rows(inverse_in[...], reach)
    for g in range(2):
        inverse[g] = inverse_groups[g]
    for p in range(points):
        for source, target in ((harden_in, harden), (modulus_in, modulus)):
            parts = split_rows(source[p], reach)
            for g in range(2):
                target[g, p] = parts[g]
        for c in range(3):
            parts = split_rows(plastic_in[c, p], reach)
            for g in range(2):
                plastic[g, c * points + p] = parts[g]

    @pl.when(has_prev)
    def _():
        rim_copy().wait_send()

    @pl.when(has_next)
    def _():
        rim_copy().wait_recv()

    rim = pl.ds(own_nodes, window)
    disp[:, rim] = jnp.where(has_next, rim_in[0], 0.0)
    vel[:, rim] = jnp.where(has_next, rim_in[1], 0.0)
    load[:, rim] = jnp.where(has_next, rim_in[2], 0.0)
    mass[:, rim] = jnp.where(has_next, STEP_TIME / rim_in[3], 0.0)

    order = list(range(reach)) + list(range(own_blocks - reach, own_blocks))
    order += list(range(reach, own_blocks - reach))
    phases = LANES // stride
    lane = lax.broadcasted_iota(jnp.int32, (ROWS, LANES), 1)

    def place_windows():
        shifted = {}
        for r in range(phases):
            for q in range(chunks - (1 if r else 0)):
                value = disp[:, cut(q)]
                if r:
                    left = LANES - r * stride
                    value = jnp.where(
                        lane < left,
                        pltpu.roll(value, left, 1),
                        pltpu.roll(disp[:, cut(q + 1)], left, 1),
                    )
                shifted[r, q] = value
        for pos, block in enumerate(order):
            for h in range(halves):
                value = shifted[block % phases, block // phases + h]
                windows[h, pos * ROWS : (pos + 1) * ROWS, :] = value

    def elements(g):
        lanes_of = [lane_at[k, g * ROWS : (g + 1) * ROWS, :] for k in range(corners)]
        halves_of = [half_at[k, g * ROWS : (g + 1) * ROWS, :] for k in range(corners)]
        corner = []
        for c in range(FREE):
            rows = [windows[h, pl.ds(g * ROWS * ROWS + c, ROWS, stride=ROWS), :] for h in range(halves)]
            values = []
            for k in range(corners):
                value = lane_take(rows[0], lanes_of[k])
                for h in range(1, halves):
                    value = jnp.where(halves_of[k] == h, lane_take(rows[h], lanes_of[k]), value)
                values.append(value)
            corner.append(values)
        z = inverse[g]
        half_z = 0.5 * z
        x = [half_z * (u[1] + u[2] - u[0] - u[3]) for u in corner]
        y = [half_z * (u[2] + u[3] - u[0] - u[1]) for u in corner]
        centre = [0.25 * (u[0] + u[1] + u[2] + u[3]) for u in corner[3:]]
        membrane = (x[0], y[1], y[0] + x[1])
        bending = (x[3], y[4], y[3] + x[4])
        transverse = (x[2] + centre[0], y[2] + centre[1])
        cost = costs[g]
        force = [jnp.zeros_like(z) for _ in range(3)]
        moment = [jnp.zeros_like(z) for _ in range(3)]
        stiff_sum = jnp.zeros_like(z)
        for p in range(points):
            young = modulus[g, p]
            old = harden[g, p]
            e = [membrane[c] + HEIGHTS[p] * bending[c] - plastic[g, c * points + p] for c in range(3)]
            stiff = young * (1.0 / (1.0 - POISSON * POISSON))
            trial = (
                stiff * (e[0] + POISSON * e[1]),
                stiff * (POISSON * e[0] + e[1]),
                stiff * (0.5 * (1.0 - POISSON)) * e[2],
            )
            first_part = trial[0] - 0.5 * trial[1]
            equal = jnp.sqrt(
                first_part * first_part + 0.75 * trial[1] * trial[1] + 3.0 * trial[2] * trial[2]
            )
            three = young * (1.5 / (1.0 + POISSON))
            decay = jnp.exp(-RATE * old)
            gap = equal - (YIELD + SATURATE)
            beyond = gap + SATURATE * decay
            change = beyond / (three + (SATURATE * RATE) * decay)
            yields = beyond > 0.0
            for turn in range(1, NEWTON):
                decay = jnp.exp(-RATE * (old + change))
                miss = gap - three * change + SATURATE * decay
                moved = change + miss / (three + (SATURATE * RATE) * decay)
                change = jnp.where(cost > turn, moved, change)
            change = jnp.where(yields & (cost > 0), change, 0.0)
            drop = three * change / jnp.maximum(equal, YIELD)
            keep = 1.0 - drop
            harden[g, p] = old + change
            for c in range(3):
                plastic[g, c * points + p] += drop * e[c]
                stress = keep * trial[c]
                force[c] = force[c] + THROUGH[p] * stress
                if HEIGHTS[p]:
                    moment[c] = moment[c] + (THROUGH[p] * HEIGHTS[p]) * stress
            stiff_sum = stiff_sum + THROUGH[p] * young
        shear = stiff_sum * (5.0 / 6.0 / (2.0 * (1.0 + POISSON)))
        q = (shear * transverse[0], shear * transverse[1])
        nx, ny, nxy = (z * v for v in force)
        mx, my, mxy = (z * v for v in moment)
        qx, qy = z * q[0], z * q[1]
        for k in range(corners):
            a, b = WEIGHT_X[k], WEIGHT_Y[k]
            values = (
                a * nx + b * nxy,
                b * ny + a * nxy,
                a * qx + b * qy,
                a * mx + b * mxy + 0.25 * q[0],
                b * my + a * mxy + 0.25 * q[1],
            )
            for c in range(FREE):
                for h in range(halves):
                    start = g * ROWS * halves * ROWS + h * ROWS + c
                    spread[k, pl.ds(start, ROWS, stride=halves * ROWS), :] = jnp.where(
                        halves_of[k] == h, values[c], 0.0
                    )

    def assemble(g):
        total = {}
        tall = halves * ROWS
        for pos in range(g * ROWS, (g + 1) * ROWS):
            block = order[pos]
            rows = jnp.concatenate(
                [spread[k, pos * tall : (pos + 1) * tall, :] for k in range(corners)], 1
            )
            high = rows.astype(jnp.bfloat16)
            low = (rows - high.astype(jnp.float32)).astype(jnp.bfloat16)
            out = lax.dot_general(
                jnp.concatenate([high, low], 0), tables[pos], (((1,), (1,)), ((), ())),
                preferred_element_type=jnp.float32,
            )
            out = out[:tall] + out[tall:]
            for h in range(halves):
                key = (block % phases, block // phases + h)
                piece = out[h * ROWS : (h + 1) * ROWS]
                total[key] = total[key] + piece if key in total else piece
        result = {}
        for (r, q), value in total.items():
            if r == 0:
                parts = ((q, value),)
            else:
                left = LANES - r * stride
                turned = pltpu.roll(value, r * stride, 1)
                parts = (
                    (q, jnp.where(lane >= r * stride, turned, 0.0)),
                    (q + 1, jnp.where(lane >= r * stride, 0.0, turned)),
                )
            for at, piece in parts:
                result[at] = result[at] + piece if at in result else piece
        return result

    pinned = (station == 0) & (member == 0)

    def forces(step, last):
        place_windows()
        elements(0)
        sums = assemble(0)
        for i in range(rim_chunks):
            ahead_out[step, :, cut(i)] = sums[own_chunks + i]
            if not last:
                back_out[step, :, cut(i)] = sums[i]

        @pl.when(has_next)
        def _():
            ahead_copy(step).start()

        if not last:
            @pl.when(has_prev)
            def _():
                back_copy(step).start()

        for q in range(chunks):
            partial[:, cut(q)] = sums.get(q, jnp.zeros((ROWS, LANES), jnp.float32))
        elements(1)

    def inner_sums():
        for q, value in assemble(1).items():
            partial[:, cut(q)] += value

    def finish(step, last):
        @pl.when(has_next)
        def _():
            ahead_copy(step).wait_send()

        @pl.when(has_prev)
        def _():
            ahead_copy(step).wait_recv()

        if not last:
            @pl.when(has_prev)
            def _():
                back_copy(step).wait_send()

            @pl.when(has_next)
            def _():
                back_copy(step).wait_recv()

        for q in range(own_chunks if last else chunks):
            internal = partial[:, cut(q)]
            if q < rim_chunks:
                internal = internal + jnp.where(has_prev, ahead_in[step, :, cut(q)], 0.0)
            if q >= own_chunks:
                internal = internal + jnp.where(
                    has_next, back_in[step, :, cut(q - own_chunks)], 0.0
                )
            speed = vel[:, cut(q)] + (load[:, cut(q)] - internal) * mass[:, cut(q)]
            if q < rim_chunks:
                speed = jnp.where(pinned, 0.0, speed)
            place = disp[:, cut(q)] + STEP_TIME * speed
            if last:
                vel_out[pl.ds(q, FREE, stride=own_chunks), :] = speed[:FREE]
                disp_out[pl.ds(q, FREE, stride=own_chunks), :] = place[:FREE]
            else:
                vel[:, cut(q)] = speed
                disp[:, cut(q)] = place

    def one_step(step, carry):
        forces(step, False)
        inner_sums()
        finish(step, False)
        return carry

    lax.fori_loop(0, STEPS - 1, one_step, 0)
    last = STEPS - 1
    forces(last, True)

    plan_column = jnp.sum(jnp.where(mine, plan_in[...], 0), axis=1, keepdims=True)
    row_at = lax.broadcasted_iota(jnp.int32, (own_blocks, own_blocks), 0)
    column_at = lax.broadcasted_iota(jnp.int32, (own_blocks, own_blocks), 1)
    plan_row = jnp.sum(jnp.where(row_at == column_at, plan_column, 0), axis=0, keepdims=True)
    rank = jnp.sum(
        jnp.where((row_at < column_at) & (plan_column == plan_row), 1, 0), axis=0, keepdims=True
    )
    slots_all = group * capacity
    slot_at = lax.broadcasted_iota(jnp.int32, (slots_all, own_blocks), 0)
    pick = jnp.where(slot_at == rank * group + plan_row, 1.0, 0.0)
    pick = jnp.concatenate([pick, pick, pick], 1).astype(jnp.bfloat16)

    def packed(ref, index):
        state = join_rows(ref[0, index], ref[1, index], reach)
        a = state.astype(jnp.bfloat16)
        rest = state - a.astype(jnp.float32)
        b = rest.astype(jnp.bfloat16)
        c = (rest - b.astype(jnp.float32)).astype(jnp.bfloat16)
        return jnp.dot(pick, jnp.concatenate([a, b, c], 0), preferred_element_type=jnp.float32)

    kinds = plastic_in.shape[0]
    fields = (kinds + 1) * points
    tall = fields * capacity
    for f in range(fields):
        rows = packed(plastic, f) if f < kinds * points else packed(harden, f - kinds * points)
        for r in range(capacity):
            pack_out[pl.ds(f * capacity + r, group, stride=tall), :] = rows[r * group : (r + 1) * group]

    def block_of(index):
        return pl.ds(pl.multiple_of(index * tall, ROWS), tall)

    def move(j):
        to = lax.rem(member + j, group)
        return pltpu.make_async_remote_copy(
            src_ref=pack_out.at[block_of(to)], dst_ref=pack_in.at[block_of(member)],
            send_sem=move_sems.at[0, j], recv_sem=move_sems.at[1, j],
            device_id=(station, to), device_id_type=MESH,
        )

    stay = pltpu.make_async_copy(
        pack_out.at[block_of(member)], pack_in.at[block_of(member)], move_sems.at[0, 0]
    )
    for j in range(1, group):
        move(j).start()
    stay.start()
    inner_sums()
    finish(last, True)
    stay.wait()
    for j in range(1, group):
        move(j).wait_send()
        move(j).wait_recv()
    for f in range(fields):
        c, p = f // points, f % points
        target = plastic_out.at[c, p] if c < kinds else harden_out.at[p]
        for r in range(capacity):
            rows = pack_in[pl.ds(f * capacity + r, group, stride=tall), :]
            target[pl.ds(r, group, stride=capacity), :] = rows


def hand_over(disp, vel, moved, hardened, disp_out, vel_out, moved_out, hardened_out, sems):
    pairs = [(disp, disp_out), (vel, vel_out), (hardened, hardened_out)]
    pairs += [(moved.at[c], moved_out.at[c]) for c in range(moved.shape[0])]
    copies = [pltpu.make_async_copy(a, b, sems.at[i]) for i, (a, b) in enumerate(pairs)]
    for copy in copies[::-1]:
        copy.start()
    for copy in copies:
        copy.wait()


def on_device(
    displacement, velocity, nodal_load, nodal_mass, plastic_strain, hardening, ply_modulus,
    inverse_size, cost_map, migration_plan, block_nodes, corner_slot,
):
    spans, group = lax.axis_size("span"), lax.axis_size("grp")
    own_nodes = displacement.shape[2]
    own_blocks, kinds, points, size = plastic_strain.shape[1:]
    window = block_nodes.shape[2]
    corners = corner_slot.shape[2]
    stride = own_nodes // own_blocks
    reach = window // stride
    capacity = max(1, (own_blocks + group - 1) // group)
    halves = window // LANES
    slots_all = group * capacity
    chunks = own_nodes + window
    f32, i32 = jnp.float32, jnp.int32
    sizes = (spans, group, own_nodes, own_blocks, window, stride, reach, capacity)
    vmem = pltpu.VMEM
    dma = pltpu.SemaphoreType.DMA
    every = pl.BlockSpec(memory_space=pltpu.MemorySpace.HBM)
    whole = pl.BlockSpec(memory_space=pltpu.VMEM)
    nodal = (displacement.shape[1] * own_nodes // LANES, LANES)
    masses = (own_nodes // LANES, LANES)
    scratch = [
        vmem(nodal, f32), vmem(nodal, f32), vmem(nodal, f32), vmem(masses, f32),
        vmem((kinds, points, own_blocks, size), f32), vmem((points, own_blocks, size), f32),
        vmem((points, own_blocks, size), f32), vmem(inverse_size.shape[1:], f32),
        vmem(cost_map.shape, i32), vmem(cost_map.shape, i32),
        vmem((own_blocks, window), i32), vmem((own_blocks, corners, size), i32),
        vmem((4, ROWS, window), f32), vmem((4, ROWS, window), f32),
        vmem((STEPS, ROWS, window), f32), vmem((STEPS, ROWS, window), f32),
        vmem((STEPS, ROWS, window), f32), vmem((STEPS, ROWS, window), f32),
        vmem((ROWS, chunks), f32), vmem((ROWS, chunks), f32),
        vmem((ROWS, chunks), f32), vmem((ROWS, chunks), f32),
        vmem((corners, own_blocks, size), i32), vmem((corners, own_blocks, size), i32),
        vmem((own_blocks, LANES, corners * size), jnp.bfloat16),
        vmem((halves, own_blocks * ROWS, LANES), f32),
        vmem((corners, own_blocks * halves * ROWS, size), f32),
        vmem((ROWS, chunks), f32),
        vmem((2, kinds * points, ROWS, size), f32), vmem((2, points, ROWS, size), f32),
        vmem((2, points, ROWS, size), f32), vmem((2, ROWS, size), f32),
        vmem((2, ROWS, size), i32),
        vmem((slots_all * (kinds + 1) * points, size), f32),
        vmem((slots_all * (kinds + 1) * points, size), f32),
        dma((12,)), dma((2,)), dma((2, STEPS)), dma((2, STEPS)), dma((2, group)),
    ]
    disp, vel, moved, hardened = pl.pallas_call(
        functools.partial(kernel, sizes),
        out_shape=(
            jax.ShapeDtypeStruct(nodal, f32),
            jax.ShapeDtypeStruct(nodal, f32),
            jax.ShapeDtypeStruct((kinds, points, slots_all, size), f32),
            jax.ShapeDtypeStruct((points, slots_all, size), f32),
        ),
        in_specs=[every] * 12,
        out_specs=(whole,) * 4,
        scratch_shapes=scratch,
        compiler_params=pltpu.CompilerParams(
            collective_id=0, has_side_effects=True, vmem_limit_bytes=63 * 1024 * 1024
        ),
    )(
        displacement.reshape(nodal), velocity.reshape(nodal), nodal_load.reshape(nodal),
        nodal_mass.reshape(masses), jnp.transpose(plastic_strain[0], (1, 2, 0, 3)),
        jnp.transpose(hardening[0], (1, 0, 2)), jnp.transpose(ply_modulus[0], (1, 0, 2)),
        inverse_size, cost_map, migration_plan.reshape(cost_map.shape), block_nodes, corner_slot,
    )
    results = (disp, vel, moved, hardened)
    disp, vel, moved, hardened = pl.pallas_call(
        hand_over,
        out_shape=tuple(jax.ShapeDtypeStruct(x.shape, f32) for x in results),
        in_specs=[every] * 4,
        out_specs=(every,) * 4,
        scratch_shapes=[dma((3 + kinds,))],
        compiler_params=pltpu.CompilerParams(vmem_limit_bytes=63 * 1024 * 1024),
    )(*results)
    return (
        disp.reshape(displacement.shape),
        vel.reshape(displacement.shape),
        jnp.transpose(moved, (2, 0, 1, 3))[None],
        jnp.transpose(hardened, (1, 0, 2))[None],
    )


def solution(mesh):
    return jax.shard_map(
        on_device,
        mesh=mesh,
        in_specs=(
            P("span", None, "grp"),
            P("span", None, "grp"),
            P("span", None, "grp"),
            P("span", "grp"),
            P("span", "grp", None, None, None),
            P("span", "grp", None, None),
            P("span", "grp", None, None),
            P("span", "grp", None),
            P("span", None),
            P("span", None, None),
            P("span", None, None),
            P("span", None, None, None),
        ),
        out_specs=(
            P("span", None, "grp"),
            P("span", None, "grp"),
            P("span", "grp", None, None, None),
            P("span", "grp", None, None),
        ),
        check_vma=False,
    )
```

```python
import functools

import jax
import jax.numpy as jnp
from jax import lax
from jax.experimental import pallas as pl
from jax.experimental.pallas import tpu as pltpu
from jax.sharding import PartitionSpec as P

NEWTON = 4
STEPS = 4

POISSON = 0.3
YIELD = 0.1
SATURATE = 0.1
RATE = 20.0
STEP_TIME = 0.25
HEIGHTS = (-0.5, -0.25, 0.0, 0.25, 0.5)
THROUGH = (1.0 / 12.0, 4.0 / 12.0, 2.0 / 12.0, 4.0 / 12.0, 1.0 / 12.0)
WEIGHT_X = (-0.5, 0.5, 0.5, -0.5)
WEIGHT_Y = (-0.5, -0.5, 0.5, 0.5)
MESH = pl.DeviceIdType.MESH
LANES = 128
ROWS = 8
FREE = 5


def pad_rows(x):
    return jnp.concatenate([x, jnp.zeros((ROWS - x.shape[0], x.shape[1]), x.dtype)], 0)


def lane_take(x, index):
    return jnp.take_along_axis(x, index, axis=1, mode="promise_in_bounds")


def split_rows(ref_rows, reach):
    return (
        jnp.concatenate([ref_rows[:reach], ref_rows[-reach:]], 0),
        ref_rows[reach:-reach],
    )


def join_rows(outer, inner, reach):
    return jnp.concatenate([outer[:reach], inner, outer[reach:]], 0)


def kernel(
    sizes,
    disp_hbm, vel_hbm, load_hbm, mass_hbm, plastic_hbm, harden_hbm, modulus_hbm, inverse_hbm,
    cost_hbm, plan_hbm, nodes_hbm, slots_hbm,
    disp_out, vel_out, plastic_out, harden_out,
    disp_in, vel_in, load_in, mass_in, plastic_in, harden_in, modulus_in, inverse_in,
    cost_in, plan_in, nodes_in, slots_in,
    rim_out, rim_in, ahead_out, ahead_in, back_out, back_in,
    disp, vel, load, mass, lane_at, half_at, tables, windows, spread, partial,
    plastic, harden, modulus, inverse, costs, pack_out, pack_in,
    in_sems, rim_sems, ahead_sems, back_sems, move_sems,
):
    spans, group, own_nodes, own_blocks, window, stride, reach, capacity = sizes
    points = harden_in.shape[0]
    corners = slots_in.shape[1]
    own_chunks = own_nodes // LANES
    rim_chunks = window // LANES
    chunks = own_chunks + rim_chunks
    station = lax.axis_index("span")
    member = lax.axis_index("grp")
    has_next = jnp.logical_not((station == spans - 1) & (member == group - 1))
    has_prev = jnp.logical_not((station == 0) & (member == 0))
    next_id = (lax.rem(station + (member + 1) // group, spans), lax.rem(member + 1, group))
    prev_id = (
        lax.rem(station + spans - 1 + (member + group - 1) // group, spans),
        lax.rem(member + group - 1, group),
    )
    outer_up = (member == group - 1) & has_next
    outer_down = (member == 0) & has_prev

    barrier = pltpu.get_barrier_semaphore()
    for j in range(1, group):
        pl.semaphore_signal(
            barrier, inc=1, device_id=(station, lax.rem(member + j, group)), device_id_type=MESH
        )

    @pl.when(outer_up)
    def _():
        pl.semaphore_signal(barrier, inc=1, device_id=next_id, device_id_type=MESH)

    @pl.when(outer_down)
    def _():
        pl.semaphore_signal(barrier, inc=1, device_id=prev_id, device_id_type=MESH)

    first = pl.multiple_of(member * own_blocks, own_blocks)
    pairs = [
        (disp_hbm, disp_in),
        (vel_hbm, vel_in),
        (load_hbm, load_in),
        (mass_hbm, mass_in),
        (plastic_hbm, plastic_in),
        (harden_hbm, harden_in),
        (modulus_hbm, modulus_in),
        (inverse_hbm.at[0], inverse_in),
        (cost_hbm, cost_in),
        (plan_hbm, plan_in),
        (nodes_hbm.at[0, pl.ds(first, own_blocks)], nodes_in),
        (slots_hbm.at[0, pl.ds(first, own_blocks)], slots_in),
    ]
    loads = [pltpu.make_async_copy(a, b, in_sems.at[i]) for i, (a, b) in enumerate(pairs)]
    for copy in loads:
        copy.start()
    for copy in loads[:4]:
        copy.wait()
    def cut(q):
        return slice(q * LANES, (q + 1) * LANES)

    def chunk(ref, q):
        return pad_rows(ref[pl.ds(q, FREE, stride=own_chunks), :])

    def mass_chunk(q):
        return jnp.broadcast_to(mass_in[q : q + 1, :], (ROWS, LANES))

    for q in range(rim_chunks):
        for i, ref in enumerate((disp_in, vel_in, load_in)):
            rim_out[i, :, cut(q)] = chunk(ref, q)
        rim_out[3, :, cut(q)] = mass_chunk(q)

    greeted = group - 1 + jnp.where(outer_up, 1, 0) + jnp.where(outer_down, 1, 0)
    pl.semaphore_wait(barrier, greeted)

    def rim_copy():
        return pltpu.make_async_remote_copy(
            src_ref=rim_out, dst_ref=rim_in, send_sem=rim_sems.at[0], recv_sem=rim_sems.at[1],
            device_id=prev_id, device_id_type=MESH,
        )

    def ahead_copy(step):
        return pltpu.make_async_remote_copy(
            src_ref=ahead_out.at[step], dst_ref=ahead_in.at[step],
            send_sem=ahead_sems.at[0, step], recv_sem=ahead_sems.at[1, step],
            device_id=next_id, device_id_type=MESH,
        )

    def back_copy(step):
        return pltpu.make_async_remote_copy(
            src_ref=back_out.at[step], dst_ref=back_in.at[step],
            send_sem=back_sems.at[0, step], recv_sem=back_sems.at[1, step],
            device_id=prev_id, device_id_type=MESH,
        )

    @pl.when(has_prev)
    def _():
        rim_copy().start()

    for q in range(own_chunks):
        for source, target in ((disp_in, disp), (vel_in, vel), (load_in, load)):
            target[:, cut(q)] = chunk(source, q)
        mass[:, cut(q)] = STEP_TIME / mass_chunk(q)
    spread[...] = jnp.zeros_like(spread)
    for copy in loads[8:]:
        copy.wait()
    node_row = lax.broadcasted_iota(jnp.int32, (own_blocks, 1), 0)
    local = nodes_in[...] - (first + node_row) * stride
    halves = window // LANES
    local_groups = split_rows(local, reach)
    for g in range(2):
        for k in range(corners):
            slot = split_rows(slots_in[:, k, :], reach)[g]
            low = slot & (LANES - 1)
            node = lane_take(local_groups[g][:, :LANES], low)
            for h in range(1, halves):
                part = lane_take(local_groups[g][:, h * LANES : (h + 1) * LANES], low)
                node = jnp.where(slot // LANES == h, part, node)
            lane_at[k, g * ROWS : (g + 1) * ROWS, :] = node & (LANES - 1)
            half_at[k, g * ROWS : (g + 1) * ROWS, :] = node // LANES
    lane_row = lax.broadcasted_iota(jnp.int32, (LANES, LANES), 0)

    def build(pos, carry):
        for k in range(corners):
            row = lane_at[k, pl.ds(pos, 1), :]
            hit = jnp.where(lane_row == row, 1.0, 0.0).astype(jnp.bfloat16)
            tables[pos, :, k * LANES : (k + 1) * LANES] = hit
        return carry

    lax.fori_loop(0, own_blocks, build, 0)

    width = cost_in.shape[1]
    at_block = lax.broadcasted_iota(jnp.int32, (own_blocks, width), 1)
    mine = at_block == first + lax.broadcasted_iota(jnp.int32, (own_blocks, width), 0)
    cost_column = jnp.sum(jnp.where(mine, cost_in[...], 0), axis=1, keepdims=True)
    cost_groups = split_rows(cost_column, reach)
    for g in range(2):
        costs[g] = jnp.broadcast_to(cost_groups[g], (ROWS, LANES))
    for copy in loads[4:8]:
        copy.wait()
    inverse_groups = split_rows(inverse_in[...], reach)
    for g in range(2):
        inverse[g] = inverse_groups[g]
    for p in range(points):
        for source, target in ((harden_in, harden), (modulus_in, modulus)):
            parts = split_rows(source[p], reach)
            for g in range(2):
                target[g, p] = parts[g]
        for c in range(3):
            parts = split_rows(plastic_in[c, p], reach)
            for g in range(2):
                plastic[g, c * points + p] = parts[g]

    @pl.when(has_prev)
    def _():
        rim_copy().wait_send()

    @pl.when(has_next)
    def _():
        rim_copy().wait_recv()

    rim = pl.ds(own_nodes, window)
    disp[:, rim] = jnp.where(has_next, rim_in[0], 0.0)
    vel[:, rim] = jnp.where(has_next, rim_in[1], 0.0)
    load[:, rim] = jnp.where(has_next, rim_in[2], 0.0)
    mass[:, rim] = jnp.where(has_next, STEP_TIME / rim_in[3], 0.0)

    order = list(range(reach)) + list(range(own_blocks - reach, own_blocks))
    order += list(range(reach, own_blocks - reach))
    phases = LANES // stride
    lane = lax.broadcasted_iota(jnp.int32, (ROWS, LANES), 1)

    def place_windows():
        shifted = {}
        for r in range(phases):
            for q in range(chunks - (1 if r else 0)):
                value = disp[:, cut(q)]
                if r:
                    left = LANES - r * stride
                    value = jnp.where(
                        lane < left,
                        pltpu.roll(value, left, 1),
                        pltpu.roll(disp[:, cut(q + 1)], left, 1),
                    )
                shifted[r, q] = value
        for pos, block in enumerate(order):
            for h in range(halves):
                value = shifted[block % phases, block // phases + h]
                windows[h, pos * ROWS : (pos + 1) * ROWS, :] = value

    def elements(g):
        lanes_of = [lane_at[k, g * ROWS : (g + 1) * ROWS, :] for k in range(corners)]
        halves_of = [half_at[k, g * ROWS : (g + 1) * ROWS, :] for k in range(corners)]
        corner = []
        for c in range(FREE):
            rows = [windows[h, pl.ds(g * ROWS * ROWS + c, ROWS, stride=ROWS), :] for h in range(halves)]
            values = []
            for k in range(corners):
                value = lane_take(rows[0], lanes_of[k])
                for h in range(1, halves):
                    value = jnp.where(halves_of[k] == h, lane_take(rows[h], lanes_of[k]), value)
                values.append(value)
            corner.append(values)
        z = inverse[g]
        half_z = 0.5 * z
        x = [half_z * (u[1] + u[2] - u[0] - u[3]) for u in corner]
        y = [half_z * (u[2] + u[3] - u[0] - u[1]) for u in corner]
        centre = [0.25 * (u[0] + u[1] + u[2] + u[3]) for u in corner[3:]]
        membrane = (x[0], y[1], y[0] + x[1])
        bending = (x[3], y[4], y[3] + x[4])
        transverse = (x[2] + centre[0], y[2] + centre[1])
        cost = costs[g]
        force = [jnp.zeros_like(z) for _ in range(3)]
        moment = [jnp.zeros_like(z) for _ in range(3)]
        stiff_sum = jnp.zeros_like(z)
        for p in range(points):
            young = modulus[g, p]
            old = harden[g, p]
            e = [membrane[c] + HEIGHTS[p] * bending[c] - plastic[g, c * points + p] for c in range(3)]
            stiff = young * (1.0 / (1.0 - POISSON * POISSON))
            trial = (
                stiff * (e[0] + POISSON * e[1]),
                stiff * (POISSON * e[0] + e[1]),
                stiff * (0.5 * (1.0 - POISSON)) * e[2],
            )
            first_part = trial[0] - 0.5 * trial[1]
            equal = jnp.sqrt(
                first_part * first_part + 0.75 * trial[1] * trial[1] + 3.0 * trial[2] * trial[2]
            )
            three = young * (1.5 / (1.0 + POISSON))
            decay = jnp.exp(-RATE * old)
            gap = equal - (YIELD + SATURATE)
            beyond = gap + SATURATE * decay
            change = beyond / (three + (SATURATE * RATE) * decay)
            yields = beyond > 0.0
            for turn in range(1, NEWTON):
                decay = jnp.exp(-RATE * (old + change))
                miss = gap - three * change + SATURATE * decay
                moved = change + miss / (three + (SATURATE * RATE) * decay)
                change = jnp.where(cost > turn, moved, change)
            change = jnp.where(yields & (cost > 0), change, 0.0)
            drop = three * change / jnp.maximum(equal, YIELD)
            keep = 1.0 - drop
            harden[g, p] = old + change
            for c in range(3):
                plastic[g, c * points + p] += drop * e[c]
                stress = keep * trial[c]
                force[c] = force[c] + THROUGH[p] * stress
                if HEIGHTS[p]:
                    moment[c] = moment[c] + (THROUGH[p] * HEIGHTS[p]) * stress
            stiff_sum = stiff_sum + THROUGH[p] * young
        shear = stiff_sum * (5.0 / 6.0 / (2.0 * (1.0 + POISSON)))
        q = (shear * transverse[0], shear * transverse[1])
        nx, ny, nxy = (z * v for v in force)
        mx, my, mxy = (z * v for v in moment)
        qx, qy = z * q[0], z * q[1]
        for k in range(corners):
            a, b = WEIGHT_X[k], WEIGHT_Y[k]
            values = (
                a * nx + b * nxy,
                b * ny + a * nxy,
                a * qx + b * qy,
                a * mx + b * mxy + 0.25 * q[0],
                b * my + a * mxy + 0.25 * q[1],
            )
            for c in range(FREE):
                for h in range(halves):
                    start = g * ROWS * halves * ROWS + h * ROWS + c
                    spread[k, pl.ds(start, ROWS, stride=halves * ROWS), :] = jnp.where(
                        halves_of[k] == h, values[c], 0.0
                    )

    def assemble(g):
        total = {}
        tall = halves * ROWS
        for pos in range(g * ROWS, (g + 1) * ROWS):
            block = order[pos]
            rows = jnp.concatenate(
                [spread[k, pos * tall : (pos + 1) * tall, :] for k in range(corners)], 1
            )
            high = rows.astype(jnp.bfloat16)
            low = (rows - high.astype(jnp.float32)).astype(jnp.bfloat16)
            out = lax.dot_general(
                jnp.concatenate([high, low], 0), tables[pos], (((1,), (1,)), ((), ())),
                preferred_element_type=jnp.float32,
            )
            out = out[:tall] + out[tall:]
            for h in range(halves):
                key = (block % phases, block // phases + h)
                piece = out[h * ROWS : (h + 1) * ROWS]
                total[key] = total[key] + piece if key in total else piece
        result = {}
        for (r, q), value in total.items():
            if r == 0:
                parts = ((q, value),)
            else:
                left = LANES - r * stride
                turned = pltpu.roll(value, r * stride, 1)
                parts = (
                    (q, jnp.where(lane >= r * stride, turned, 0.0)),
                    (q + 1, jnp.where(lane >= r * stride, 0.0, turned)),
                )
            for at, piece in parts:
                result[at] = result[at] + piece if at in result else piece
        return result

    pinned = (station == 0) & (member == 0)

    def forces(step, last):
        place_windows()
        elements(0)
        sums = assemble(0)
        for i in range(rim_chunks):
            ahead_out[step, :, cut(i)] = sums[own_chunks + i]
            if not last:
                back_out[step, :, cut(i)] = sums[i]

        @pl.when(has_next)
        def _():
            ahead_copy(step).start()

        if not last:
            @pl.when(has_prev)
            def _():
                back_copy(step).start()

        for q in range(chunks):
            partial[:, cut(q)] = sums.get(q, jnp.zeros((ROWS, LANES), jnp.float32))
        elements(1)

    def inner_sums():
        for q, value in assemble(1).items():
            partial[:, cut(q)] += value

    def finish(step, last):
        @pl.when(has_next)
        def _():
            ahead_copy(step).wait_send()

        @pl.when(has_prev)
        def _():
            ahead_copy(step).wait_recv()

        if not last:
            @pl.when(has_prev)
            def _():
                back_copy(step).wait_send()

            @pl.when(has_next)
            def _():
                back_copy(step).wait_recv()

        for q in range(own_chunks if last else chunks):
            internal = partial[:, cut(q)]
            if q < rim_chunks:
                internal = internal + jnp.where(has_prev, ahead_in[step, :, cut(q)], 0.0)
            if q >= own_chunks:
                internal = internal + jnp.where(
                    has_next, back_in[step, :, cut(q - own_chunks)], 0.0
                )
            speed = vel[:, cut(q)] + (load[:, cut(q)] - internal) * mass[:, cut(q)]
            if q < rim_chunks:
                speed = jnp.where(pinned, 0.0, speed)
            place = disp[:, cut(q)] + STEP_TIME * speed
            if last:
                vel_out[pl.ds(q, FREE, stride=own_chunks), :] = speed[:FREE]
                disp_out[pl.ds(q, FREE, stride=own_chunks), :] = place[:FREE]
            else:
                vel[:, cut(q)] = speed
                disp[:, cut(q)] = place

    def one_step(step, carry):
        forces(step, False)
        inner_sums()
        finish(step, False)
        return carry

    lax.fori_loop(0, STEPS - 1, one_step, 0)
    last = STEPS - 1
    forces(last, True)

    plan_column = jnp.sum(jnp.where(mine, plan_in[...], 0), axis=1, keepdims=True)
    row_at = lax.broadcasted_iota(jnp.int32, (own_blocks, own_blocks), 0)
    column_at = lax.broadcasted_iota(jnp.int32, (own_blocks, own_blocks), 1)
    plan_row = jnp.sum(jnp.where(row_at == column_at, plan_column, 0), axis=0, keepdims=True)
    rank = jnp.sum(
        jnp.where((row_at < column_at) & (plan_column == plan_row), 1, 0), axis=0, keepdims=True
    )
    slots_all = group * capacity
    slot_at = lax.broadcasted_iota(jnp.int32, (slots_all, own_blocks), 0)
    pick = jnp.where(slot_at == rank * group + plan_row, 1.0, 0.0)
    pick = jnp.concatenate([pick, pick, pick], 1).astype(jnp.bfloat16)

    def packed(ref, index):
        state = join_rows(ref[0, index], ref[1, index], reach)
        a = state.astype(jnp.bfloat16)
        rest = state - a.astype(jnp.float32)
        b = rest.astype(jnp.bfloat16)
        c = (rest - b.astype(jnp.float32)).astype(jnp.bfloat16)
        return jnp.dot(pick, jnp.concatenate([a, b, c], 0), preferred_element_type=jnp.float32)

    kinds = plastic_in.shape[0]
    fields = (kinds + 1) * points
    tall = fields * capacity
    for f in range(fields):
        rows = packed(plastic, f) if f < kinds * points else packed(harden, f - kinds * points)
        for r in range(capacity):
            pack_out[pl.ds(f * capacity + r, group, stride=tall), :] = rows[r * group : (r + 1) * group]

    def block_of(index):
        return pl.ds(pl.multiple_of(index * tall, ROWS), tall)

    def move(j):
        to = lax.rem(member + j, group)
        return pltpu.make_async_remote_copy(
            src_ref=pack_out.at[block_of(to)], dst_ref=pack_in.at[block_of(member)],
            send_sem=move_sems.at[0, j], recv_sem=move_sems.at[1, j],
            device_id=(station, to), device_id_type=MESH,
        )

    stay = pltpu.make_async_copy(
        pack_out.at[block_of(member)], pack_in.at[block_of(member)], move_sems.at[0, 0]
    )
    for j in range(1, group):
        move(j).start()
    stay.start()
    inner_sums()
    finish(last, True)
    stay.wait()
    for j in range(1, group):
        move(j).wait_send()
        move(j).wait_recv()
    for f in range(fields):
        c, p = f // points, f % points
        target = plastic_out.at[c, p] if c < kinds else harden_out.at[p]
        for r in range(capacity):
            rows = pack_in[pl.ds(f * capacity + r, group, stride=tall), :]
            target[pl.ds(r, group, stride=capacity), :] = rows


def hand_over(disp, vel, moved, hardened, disp_out, vel_out, moved_out, hardened_out, sems):
    pairs = [(disp, disp_out), (vel, vel_out), (hardened, hardened_out)]
    pairs += [(moved.at[c], moved_out.at[c]) for c in range(moved.shape[0])]
    copies = [pltpu.make_async_copy(a, b, sems.at[i]) for i, (a, b) in enumerate(pairs)]
    for copy in copies[::-1]:
        copy.start()
    for copy in copies:
        copy.wait()


def on_device(
    displacement, velocity, nodal_load, nodal_mass, plastic_strain, hardening, ply_modulus,
    inverse_size, cost_map, migration_plan, block_nodes, corner_slot,
):
    spans, group = lax.axis_size("span"), lax.axis_size("grp")
    own_nodes = displacement.shape[2]
    own_blocks, kinds, points, size = plastic_strain.shape[1:]
    window = block_nodes.shape[2]
    corners = corner_slot.shape[2]
    stride = own_nodes // own_blocks
    reach = window // stride
    capacity = max(1, (own_blocks + group - 1) // group)
    halves = window // LANES
    slots_all = group * capacity
    chunks = own_nodes + window
    f32, i32 = jnp.float32, jnp.int32
    sizes = (spans, group, own_nodes, own_blocks, window, stride, reach, capacity)
    vmem = pltpu.VMEM
    dma = pltpu.SemaphoreType.DMA
    every = pl.BlockSpec(memory_space=pltpu.MemorySpace.HBM)
    whole = pl.BlockSpec(memory_space=pltpu.VMEM)
    nodal = (displacement.shape[1] * own_nodes // LANES, LANES)
    masses = (own_nodes // LANES, LANES)
    scratch = [
        vmem(nodal, f32), vmem(nodal, f32), vmem(nodal, f32), vmem(masses, f32),
        vmem((kinds, points, own_blocks, size), f32), vmem((points, own_blocks, size), f32),
        vmem((points, own_blocks, size), f32), vmem(inverse_size.shape[1:], f32),
        vmem(cost_map.shape, i32), vmem(cost_map.shape, i32),
        vmem((own_blocks, window), i32), vmem((own_blocks, corners, size), i32),
        vmem((4, ROWS, window), f32), vmem((4, ROWS, window), f32),
        vmem((STEPS, ROWS, window), f32), vmem((STEPS, ROWS, window), f32),
        vmem((STEPS, ROWS, window), f32), vmem((STEPS, ROWS, window), f32),
        vmem((ROWS, chunks), f32), vmem((ROWS, chunks), f32),
        vmem((ROWS, chunks), f32), vmem((ROWS, chunks), f32),
        vmem((corners, own_blocks, size), i32), vmem((corners, own_blocks, size), i32),
        vmem((own_blocks, LANES, corners * size), jnp.bfloat16),
        vmem((halves, own_blocks * ROWS, LANES), f32),
        vmem((corners, own_blocks * halves * ROWS, size), f32),
        vmem((ROWS, chunks), f32),
        vmem((2, kinds * points, ROWS, size), f32), vmem((2, points, ROWS, size), f32),
        vmem((2, points, ROWS, size), f32), vmem((2, ROWS, size), f32),
        vmem((2, ROWS, size), i32),
        vmem((slots_all * (kinds + 1) * points, size), f32),
        vmem((slots_all * (kinds + 1) * points, size), f32),
        dma((12,)), dma((2,)), dma((2, STEPS)), dma((2, STEPS)), dma((2, group)),
    ]
    disp, vel, moved, hardened = pl.pallas_call(
        functools.partial(kernel, sizes),
        out_shape=(
            jax.ShapeDtypeStruct(nodal, f32),
            jax.ShapeDtypeStruct(nodal, f32),
            jax.ShapeDtypeStruct((kinds, points, slots_all, size), f32),
            jax.ShapeDtypeStruct((points, slots_all, size), f32),
        ),
        in_specs=[every] * 12,
        out_specs=(whole,) * 4,
        scratch_shapes=scratch,
        compiler_params=pltpu.CompilerParams(
            collective_id=0, has_side_effects=True, vmem_limit_bytes=63 * 1024 * 1024
        ),
    )(
        displacement.reshape(nodal), velocity.reshape(nodal), nodal_load.reshape(nodal),
        nodal_mass.reshape(masses), jnp.transpose(plastic_strain[0], (1, 2, 0, 3)),
        jnp.transpose(hardening[0], (1, 0, 2)), jnp.transpose(ply_modulus[0], (1, 0, 2)),
        inverse_size, cost_map, migration_plan.reshape(cost_map.shape), block_nodes, corner_slot,
    )
    results = (disp, vel, moved, hardened)
    disp, vel, moved, hardened = pl.pallas_call(
        hand_over,
        out_shape=tuple(jax.ShapeDtypeStruct(x.shape, f32) for x in results),
        in_specs=[whole] * 4,
        out_specs=(every,) * 4,
        scratch_shapes=[dma((3 + kinds,))],
        compiler_params=pltpu.CompilerParams(vmem_limit_bytes=63 * 1024 * 1024),
    )(*results)
    return (
        disp.reshape(displacement.shape),
        vel.reshape(displacement.shape),
        jnp.transpose(moved, (2, 0, 1, 3))[None],
        jnp.transpose(hardened, (1, 0, 2))[None],
    )


def solution(mesh):
    return jax.shard_map(
        on_device,
        mesh=mesh,
        in_specs=(
            P("span", None, "grp"),
            P("span", None, "grp"),
            P("span", None, "grp"),
            P("span", "grp"),
            P("span", "grp", None, None, None),
            P("span", "grp", None, None),
            P("span", "grp", None, None),
            P("span", "grp", None),
            P("span", None),
            P("span", None, None),
            P("span", None, None),
            P("span", None, None, None),
        ),
        out_specs=(
            P("span", None, "grp"),
            P("span", None, "grp"),
            P("span", "grp", None, None, None),
            P("span", "grp", None, None),
        ),
        check_vma=False,
    )
```

```python
import functools

import jax
import jax.numpy as jnp
from jax import lax
from jax.experimental import pallas as pl
from jax.experimental.pallas import tpu as pltpu
from jax.sharding import PartitionSpec as P

NEWTON = 4
STEPS = 4

POISSON = 0.3
YIELD = 0.1
SATURATE = 0.1
RATE = 20.0
STEP_TIME = 0.25
HEIGHTS = (-0.5, -0.25, 0.0, 0.25, 0.5)
THROUGH = (1.0 / 12.0, 4.0 / 12.0, 2.0 / 12.0, 4.0 / 12.0, 1.0 / 12.0)
WEIGHT_X = (-0.5, 0.5, 0.5, -0.5)
WEIGHT_Y = (-0.5, -0.5, 0.5, 0.5)
MESH = pl.DeviceIdType.MESH
LANES = 128
ROWS = 8
FREE = 5


def pad_rows(x):
    return jnp.concatenate([x, jnp.zeros((ROWS - x.shape[0], x.shape[1]), x.dtype)], 0)


def lane_take(x, index):
    return jnp.take_along_axis(x, index, axis=1, mode="promise_in_bounds")


def quotient(x, y):
    guess = pl.reciprocal(y, approx=True)
    return x * (guess * (2.0 - y * guess))


def split_rows(ref_rows, reach):
    return (
        jnp.concatenate([ref_rows[:reach], ref_rows[-reach:]], 0),
        ref_rows[reach:-reach],
    )


def join_rows(outer, inner, reach):
    return jnp.concatenate([outer[:reach], inner, outer[reach:]], 0)


def kernel(
    sizes,
    disp_hbm, vel_hbm, load_hbm, mass_hbm, plastic_hbm, harden_hbm, modulus_hbm, inverse_hbm,
    cost_hbm, plan_hbm, nodes_hbm, slots_hbm,
    disp_out, vel_out, plastic_out, harden_out,
    disp_in, vel_in, load_in, mass_in, plastic_in, harden_in, modulus_in, inverse_in,
    cost_in, plan_in, nodes_in, slots_in,
    rim_out, rim_in, ahead_out, ahead_in, back_out, back_in,
    disp, vel, load, mass, lane_at, half_at, tables, windows, spread, partial,
    plastic, harden, modulus, inverse, costs, pack_out, pack_in,
    in_sems, rim_sems, ahead_sems, back_sems, move_sems,
):
    spans, group, own_nodes, own_blocks, window, stride, reach, capacity = sizes
    points = harden_in.shape[0]
    corners = slots_in.shape[1]
    own_chunks = own_nodes // LANES
    rim_chunks = window // LANES
    chunks = own_chunks + rim_chunks
    station = lax.axis_index("span")
    member = lax.axis_index("grp")
    has_next = jnp.logical_not((station == spans - 1) & (member == group - 1))
    has_prev = jnp.logical_not((station == 0) & (member == 0))
    next_id = (lax.rem(station + (member + 1) // group, spans), lax.rem(member + 1, group))
    prev_id = (
        lax.rem(station + spans - 1 + (member + group - 1) // group, spans),
        lax.rem(member + group - 1, group),
    )
    outer_up = (member == group - 1) & has_next
    outer_down = (member == 0) & has_prev

    barrier = pltpu.get_barrier_semaphore()
    for j in range(1, group):
        pl.semaphore_signal(
            barrier, inc=1, device_id=(station, lax.rem(member + j, group)), device_id_type=MESH
        )

    @pl.when(outer_up)
    def _():
        pl.semaphore_signal(barrier, inc=1, device_id=next_id, device_id_type=MESH)

    @pl.when(outer_down)
    def _():
        pl.semaphore_signal(barrier, inc=1, device_id=prev_id, device_id_type=MESH)

    first = pl.multiple_of(member * own_blocks, own_blocks)
    pairs = [
        (disp_hbm, disp_in),
        (vel_hbm, vel_in),
        (load_hbm, load_in),
        (mass_hbm, mass_in),
        (plastic_hbm, plastic_in),
        (harden_hbm, harden_in),
        (modulus_hbm, modulus_in),
        (inverse_hbm.at[0], inverse_in),
        (cost_hbm, cost_in),
        (plan_hbm, plan_in),
        (nodes_hbm.at[0, pl.ds(first, own_blocks)], nodes_in),
        (slots_hbm.at[0, pl.ds(first, own_blocks)], slots_in),
    ]
    loads = [pltpu.make_async_copy(a, b, in_sems.at[i]) for i, (a, b) in enumerate(pairs)]
    for copy in loads:
        copy.start()
    for copy in loads[:4]:
        copy.wait()
    def cut(q):
        return slice(q * LANES, (q + 1) * LANES)

    def chunk(ref, q):
        return pad_rows(ref[pl.ds(q, FREE, stride=own_chunks), :])

    def mass_chunk(q):
        return jnp.broadcast_to(mass_in[q : q + 1, :], (ROWS, LANES))

    for q in range(rim_chunks):
        for i, ref in enumerate((disp_in, vel_in, load_in)):
            rim_out[i, :, cut(q)] = chunk(ref, q)
        rim_out[3, :, cut(q)] = mass_chunk(q)

    greeted = group - 1 + jnp.where(outer_up, 1, 0) + jnp.where(outer_down, 1, 0)
    pl.semaphore_wait(barrier, greeted)

    def rim_copy():
        return pltpu.make_async_remote_copy(
            src_ref=rim_out, dst_ref=rim_in, send_sem=rim_sems.at[0], recv_sem=rim_sems.at[1],
            device_id=prev_id, device_id_type=MESH,
        )

    def ahead_copy(step):
        return pltpu.make_async_remote_copy(
            src_ref=ahead_out.at[step], dst_ref=ahead_in.at[step],
            send_sem=ahead_sems.at[0, step], recv_sem=ahead_sems.at[1, step],
            device_id=next_id, device_id_type=MESH,
        )

    def back_copy(step):
        return pltpu.make_async_remote_copy(
            src_ref=back_out.at[step], dst_ref=back_in.at[step],
            send_sem=back_sems.at[0, step], recv_sem=back_sems.at[1, step],
            device_id=prev_id, device_id_type=MESH,
        )

    @pl.when(has_prev)
    def _():
        rim_copy().start()

    for q in range(own_chunks):
        for source, target in ((disp_in, disp), (vel_in, vel), (load_in, load)):
            target[:, cut(q)] = chunk(source, q)
        mass[:, cut(q)] = STEP_TIME / mass_chunk(q)
    spread[...] = jnp.zeros_like(spread)
    for copy in loads[8:]:
        copy.wait()
    node_row = lax.broadcasted_iota(jnp.int32, (own_blocks, 1), 0)
    local = nodes_in[...] - (first + node_row) * stride
    halves = window // LANES
    local_groups = split_rows(local, reach)
    for g in range(2):
        for k in range(corners):
            slot = split_rows(slots_in[:, k, :], reach)[g]
            low = slot & (LANES - 1)
            node = lane_take(local_groups[g][:, :LANES], low)
            for h in range(1, halves):
                part = lane_take(local_groups[g][:, h * LANES : (h + 1) * LANES], low)
                node = jnp.where(slot // LANES == h, part, node)
            lane_at[k, g * ROWS : (g + 1) * ROWS, :] = node & (LANES - 1)
            half_at[k, g * ROWS : (g + 1) * ROWS, :] = node // LANES
    lane_row = lax.broadcasted_iota(jnp.int32, (LANES, LANES), 0)

    def build(pos, carry):
        for k in range(corners):
            row = lane_at[k, pl.ds(pos, 1), :]
            hit = jnp.where(lane_row == row, 1.0, 0.0).astype(jnp.bfloat16)
            tables[pos, :, k * LANES : (k + 1) * LANES] = hit
        return carry

    lax.fori_loop(0, own_blocks, build, 0)

    width = cost_in.shape[1]
    at_block = lax.broadcasted_iota(jnp.int32, (own_blocks, width), 1)
    mine = at_block == first + lax.broadcasted_iota(jnp.int32, (own_blocks, width), 0)
    cost_column = jnp.sum(jnp.where(mine, cost_in[...], 0), axis=1, keepdims=True)
    cost_groups = split_rows(cost_column, reach)
    for g in range(2):
        costs[g] = jnp.broadcast_to(cost_groups[g], (ROWS, LANES))
    for copy in loads[4:8]:
        copy.wait()
    inverse_groups = split_rows(inverse_in[...], reach)
    for g in range(2):
        inverse[g] = inverse_groups[g]
    for p in range(points):
        for source, target in ((harden_in, harden), (modulus_in, modulus)):
            parts = split_rows(source[p], reach)
            for g in range(2):
                target[g, p] = parts[g]
        for c in range(3):
            parts = split_rows(plastic_in[c, p], reach)
            for g in range(2):
                plastic[g, c * points + p] = parts[g]

    @pl.when(has_prev)
    def _():
        rim_copy().wait_send()

    @pl.when(has_next)
    def _():
        rim_copy().wait_recv()

    rim = pl.ds(own_nodes, window)
    disp[:, rim] = jnp.where(has_next, rim_in[0], 0.0)
    vel[:, rim] = jnp.where(has_next, rim_in[1], 0.0)
    load[:, rim] = jnp.where(has_next, rim_in[2], 0.0)
    mass[:, rim] = jnp.where(has_next, STEP_TIME / rim_in[3], 0.0)

    order = list(range(reach)) + list(range(own_blocks - reach, own_blocks))
    order += list(range(reach, own_blocks - reach))
    phases = LANES // stride
    lane = lax.broadcasted_iota(jnp.int32, (ROWS, LANES), 1)

    def place_windows():
        shifted = {}
        for r in range(phases):
            for q in range(chunks - (1 if r else 0)):
                value = disp[:, cut(q)]
                if r:
                    left = LANES - r * stride
                    value = jnp.where(
                        lane < left,
                        pltpu.roll(value, left, 1),
                        pltpu.roll(disp[:, cut(q + 1)], left, 1),
                    )
                shifted[r, q] = value
        for pos, block in enumerate(order):
            for h in range(halves):
                value = shifted[block % phases, block // phases + h]
                windows[h, pos * ROWS : (pos + 1) * ROWS, :] = value

    def elements(g):
        lanes_of = [lane_at[k, g * ROWS : (g + 1) * ROWS, :] for k in range(corners)]
        halves_of = [half_at[k, g * ROWS : (g + 1) * ROWS, :] for k in range(corners)]
        corner = []
        for c in range(FREE):
            rows = [windows[h, pl.ds(g * ROWS * ROWS + c, ROWS, stride=ROWS), :] for h in range(halves)]
            values = []
            for k in range(corners):
                value = lane_take(rows[0], lanes_of[k])
                for h in range(1, halves):
                    value = jnp.where(halves_of[k] == h, lane_take(rows[h], lanes_of[k]), value)
                values.append(value)
            corner.append(values)
        z = inverse[g]
        half_z = 0.5 * z
        x = [half_z * (u[1] + u[2] - u[0] - u[3]) for u in corner]
        y = [half_z * (u[2] + u[3] - u[0] - u[1]) for u in corner]
        centre = [0.25 * (u[0] + u[1] + u[2] + u[3]) for u in corner[3:]]
        membrane = (x[0], y[1], y[0] + x[1])
        bending = (x[3], y[4], y[3] + x[4])
        transverse = (x[2] + centre[0], y[2] + centre[1])
        cost = costs[g]
        force = [jnp.zeros_like(z) for _ in range(3)]
        moment = [jnp.zeros_like(z) for _ in range(3)]
        stiff_sum = jnp.zeros_like(z)
        for p in range(points):
            young = modulus[g, p]
            old = harden[g, p]
            e = [membrane[c] + HEIGHTS[p] * bending[c] - plastic[g, c * points + p] for c in range(3)]
            stiff = young * (1.0 / (1.0 - POISSON * POISSON))
            trial = (
                stiff * (e[0] + POISSON * e[1]),
                stiff * (POISSON * e[0] + e[1]),
                stiff * (0.5 * (1.0 - POISSON)) * e[2],
            )
            first_part = trial[0] - 0.5 * trial[1]
            equal = jnp.sqrt(
                first_part * first_part + 0.75 * trial[1] * trial[1] + 3.0 * trial[2] * trial[2]
            )
            three = young * (1.5 / (1.0 + POISSON))
            decay = jnp.exp(-RATE * old)
            gap = equal - (YIELD + SATURATE)
            beyond = gap + SATURATE * decay
            change = quotient(beyond, three + (SATURATE * RATE) * decay)
            yields = beyond > 0.0
            for turn in range(1, NEWTON):
                decay = jnp.exp(-RATE * (old + change))
                miss = gap - three * change + SATURATE * decay
                moved = change + quotient(miss, three + (SATURATE * RATE) * decay)
                change = jnp.where(cost > turn, moved, change)
            change = jnp.where(yields & (cost > 0), change, 0.0)
            drop = quotient(three * change, jnp.maximum(equal, YIELD))
            keep = 1.0 - drop
            harden[g, p] = old + change
            for c in range(3):
                plastic[g, c * points + p] += drop * e[c]
                stress = keep * trial[c]
                force[c] = force[c] + THROUGH[p] * stress
                if HEIGHTS[p]:
                    moment[c] = moment[c] + (THROUGH[p] * HEIGHTS[p]) * stress
            stiff_sum = stiff_sum + THROUGH[p] * young
        shear = stiff_sum * (5.0 / 6.0 / (2.0 * (1.0 + POISSON)))
        q = (shear * transverse[0], shear * transverse[1])
        nx, ny, nxy = (z * v for v in force)
        mx, my, mxy = (z * v for v in moment)
        qx, qy = z * q[0], z * q[1]
        for k in range(corners):
            a, b = WEIGHT_X[k], WEIGHT_Y[k]
            values = (
                a * nx + b * nxy,
                b * ny + a * nxy,
                a * qx + b * qy,
                a * mx + b * mxy + 0.25 * q[0],
                b * my + a * mxy + 0.25 * q[1],
            )
            for c in range(FREE):
                for h in range(halves):
                    start = g * ROWS * halves * ROWS + h * ROWS + c
                    spread[k, pl.ds(start, ROWS, stride=halves * ROWS), :] = jnp.where(
                        halves_of[k] == h, values[c], 0.0
                    )

    def assemble(g):
        total = {}
        tall = halves * ROWS
        for pos in range(g * ROWS, (g + 1) * ROWS):
            block = order[pos]
            rows = jnp.concatenate(
                [spread[k, pos * tall : (pos + 1) * tall, :] for k in range(corners)], 1
            )
            high = rows.astype(jnp.bfloat16)
            low = (rows - high.astype(jnp.float32)).astype(jnp.bfloat16)
            out = lax.dot_general(
                jnp.concatenate([high, low], 0), tables[pos], (((1,), (1,)), ((), ())),
                preferred_element_type=jnp.float32,
            )
            out = out[:tall] + out[tall:]
            for h in range(halves):
                key = (block % phases, block // phases + h)
                piece = out[h * ROWS : (h + 1) * ROWS]
                total[key] = total[key] + piece if key in total else piece
        result = {}
        for (r, q), value in total.items():
            if r == 0:
                parts = ((q, value),)
            else:
                left = LANES - r * stride
                turned = pltpu.roll(value, r * stride, 1)
                parts = (
                    (q, jnp.where(lane >= r * stride, turned, 0.0)),
                    (q + 1, jnp.where(lane >= r * stride, 0.0, turned)),
                )
            for at, piece in parts:
                result[at] = result[at] + piece if at in result else piece
        return result

    pinned = (station == 0) & (member == 0)

    def outer_sums(step, last):
        sums = assemble(0)
        for i in range(rim_chunks):
            ahead_out[step, :, cut(i)] = sums[own_chunks + i]
            if not last:
                back_out[step, :, cut(i)] = sums[i]

        @pl.when(has_next)
        def _():
            ahead_copy(step).start()

        if not last:
            @pl.when(has_prev)
            def _():
                back_copy(step).start()

        for q in range(chunks):
            partial[:, cut(q)] = sums.get(q, jnp.zeros((ROWS, LANES), jnp.float32))

    def inner_sums():
        for q, value in assemble(1).items():
            partial[:, cut(q)] += value

    def finish(step, last):
        @pl.when(has_next)
        def _():
            ahead_copy(step).wait_send()

        @pl.when(has_prev)
        def _():
            ahead_copy(step).wait_recv()

        if not last:
            @pl.when(has_prev)
            def _():
                back_copy(step).wait_send()

            @pl.when(has_next)
            def _():
                back_copy(step).wait_recv()

        for q in range(own_chunks if last else chunks):
            internal = partial[:, cut(q)]
            if q < rim_chunks:
                internal = internal + jnp.where(has_prev, ahead_in[step, :, cut(q)], 0.0)
            if q >= own_chunks:
                internal = internal + jnp.where(
                    has_next, back_in[step, :, cut(q - own_chunks)], 0.0
                )
            speed = vel[:, cut(q)] + (load[:, cut(q)] - internal) * mass[:, cut(q)]
            if q < rim_chunks:
                speed = jnp.where(pinned, 0.0, speed)
            place = disp[:, cut(q)] + STEP_TIME * speed
            if last:
                vel_out[pl.ds(q, FREE, stride=own_chunks), :] = speed[:FREE]
                disp_out[pl.ds(q, FREE, stride=own_chunks), :] = place[:FREE]
            else:
                vel[:, cut(q)] = speed
                disp[:, cut(q)] = place

    def one_step(step, carry):
        place_windows()
        elements(0)
        outer_sums(step, False)
        elements(1)
        inner_sums()
        finish(step, False)
        return carry

    lax.fori_loop(0, STEPS - 1, one_step, 0)
    last = STEPS - 1
    place_windows()
    elements(0)
    elements(1)

    plan_column = jnp.sum(jnp.where(mine, plan_in[...], 0), axis=1, keepdims=True)
    row_at = lax.broadcasted_iota(jnp.int32, (own_blocks, own_blocks), 0)
    column_at = lax.broadcasted_iota(jnp.int32, (own_blocks, own_blocks), 1)
    plan_row = jnp.sum(jnp.where(row_at == column_at, plan_column, 0), axis=0, keepdims=True)
    rank = jnp.sum(
        jnp.where((row_at < column_at) & (plan_column == plan_row), 1, 0), axis=0, keepdims=True
    )
    slots_all = group * capacity
    slot_at = lax.broadcasted_iota(jnp.int32, (slots_all, own_blocks), 0)
    pick = jnp.where(slot_at == rank * group + plan_row, 1.0, 0.0)
    pick = jnp.concatenate([pick, pick, pick], 1).astype(jnp.bfloat16)

    def packed(ref, index):
        state = join_rows(ref[0, index], ref[1, index], reach)
        a = state.astype(jnp.bfloat16)
        rest = state - a.astype(jnp.float32)
        b = rest.astype(jnp.bfloat16)
        c = (rest - b.astype(jnp.float32)).astype(jnp.bfloat16)
        return jnp.dot(pick, jnp.concatenate([a, b, c], 0), preferred_element_type=jnp.float32)

    kinds = plastic_in.shape[0]
    fields = (kinds + 1) * points
    tall = fields * capacity
    for f in range(fields):
        rows = packed(plastic, f) if f < kinds * points else packed(harden, f - kinds * points)
        for r in range(capacity):
            pack_out[pl.ds(f * capacity + r, group, stride=tall), :] = rows[r * group : (r + 1) * group]

    def block_of(index):
        return pl.ds(pl.multiple_of(index * tall, ROWS), tall)

    def move(j):
        to = lax.rem(member + j, group)
        return pltpu.make_async_remote_copy(
            src_ref=pack_out.at[block_of(to)], dst_ref=pack_in.at[block_of(member)],
            send_sem=move_sems.at[0, j], recv_sem=move_sems.at[1, j],
            device_id=(station, to), device_id_type=MESH,
        )

    stay = pltpu.make_async_copy(
        pack_out.at[block_of(member)], pack_in.at[block_of(member)], move_sems.at[0, 0]
    )
    for j in range(1, group):
        move(j).start()
    outer_sums(last, True)
    stay.start()
    inner_sums()
    finish(last, True)
    stay.wait()
    for j in range(1, group):
        move(j).wait_send()
        move(j).wait_recv()
    for f in range(fields):
        c, p = f // points, f % points
        target = plastic_out.at[c, p] if c < kinds else harden_out.at[p]
        for r in range(capacity):
            rows = pack_in[pl.ds(f * capacity + r, group, stride=tall), :]
            target[pl.ds(r, group, stride=capacity), :] = rows


def hand_over(disp, vel, moved, hardened, disp_out, vel_out, moved_out, hardened_out, sems):
    pairs = [(disp, disp_out), (vel, vel_out), (hardened, hardened_out)]
    pairs += [(moved.at[c], moved_out.at[c]) for c in range(moved.shape[0])]
    copies = [pltpu.make_async_copy(a, b, sems.at[i]) for i, (a, b) in enumerate(pairs)]
    for copy in copies[::-1]:
        copy.start()
    for copy in copies:
        copy.wait()


def on_device(
    displacement, velocity, nodal_load, nodal_mass, plastic_strain, hardening, ply_modulus,
    inverse_size, cost_map, migration_plan, block_nodes, corner_slot,
):
    spans, group = lax.axis_size("span"), lax.axis_size("grp")
    own_nodes = displacement.shape[2]
    own_blocks, kinds, points, size = plastic_strain.shape[1:]
    window = block_nodes.shape[2]
    corners = corner_slot.shape[2]
    stride = own_nodes // own_blocks
    reach = window // stride
    capacity = max(1, (own_blocks + group - 1) // group)
    halves = window // LANES
    slots_all = group * capacity
    chunks = own_nodes + window
    f32, i32 = jnp.float32, jnp.int32
    sizes = (spans, group, own_nodes, own_blocks, window, stride, reach, capacity)
    vmem = pltpu.VMEM
    dma = pltpu.SemaphoreType.DMA
    every = pl.BlockSpec(memory_space=pltpu.MemorySpace.HBM)
    whole = pl.BlockSpec(memory_space=pltpu.VMEM)
    nodal = (displacement.shape[1] * own_nodes // LANES, LANES)
    masses = (own_nodes // LANES, LANES)
    scratch = [
        vmem(nodal, f32), vmem(nodal, f32), vmem(nodal, f32), vmem(masses, f32),
        vmem((kinds, points, own_blocks, size), f32), vmem((points, own_blocks, size), f32),
        vmem((points, own_blocks, size), f32), vmem(inverse_size.shape[1:], f32),
        vmem(cost_map.shape, i32), vmem(cost_map.shape, i32),
        vmem((own_blocks, window), i32), vmem((own_blocks, corners, size), i32),
        vmem((4, ROWS, window), f32), vmem((4, ROWS, window), f32),
        vmem((STEPS, ROWS, window), f32), vmem((STEPS, ROWS, window), f32),
        vmem((STEPS, ROWS, window), f32), vmem((STEPS, ROWS, window), f32),
        vmem((ROWS, chunks), f32), vmem((ROWS, chunks), f32),
        vmem((ROWS, chunks), f32), vmem((ROWS, chunks), f32),
        vmem((corners, own_blocks, size), i32), vmem((corners, own_blocks, size), i32),
        vmem((own_blocks, LANES, corners * size), jnp.bfloat16),
        vmem((halves, own_blocks * ROWS, LANES), f32),
        vmem((corners, own_blocks * halves * ROWS, size), f32),
        vmem((ROWS, chunks), f32),
        vmem((2, kinds * points, ROWS, size), f32), vmem((2, points, ROWS, size), f32),
        vmem((2, points, ROWS, size), f32), vmem((2, ROWS, size), f32),
        vmem((2, ROWS, size), i32),
        vmem((slots_all * (kinds + 1) * points, size), f32),
        vmem((slots_all * (kinds + 1) * points, size), f32),
        dma((12,)), dma((2,)), dma((2, STEPS)), dma((2, STEPS)), dma((2, group)),
    ]
    disp, vel, moved, hardened = pl.pallas_call(
        functools.partial(kernel, sizes),
        out_shape=(
            vmem(nodal, f32),
            vmem(nodal, f32),
            vmem((kinds, points, slots_all, size), f32),
            vmem((points, slots_all, size), f32),
        ),
        in_specs=[every] * 12,
        out_specs=(whole,) * 4,
        scratch_shapes=scratch,
        compiler_params=pltpu.CompilerParams(
            collective_id=0, has_side_effects=True, vmem_limit_bytes=63 * 1024 * 1024
        ),
    )(
        displacement.reshape(nodal), velocity.reshape(nodal), nodal_load.reshape(nodal),
        nodal_mass.reshape(masses), jnp.transpose(plastic_strain[0], (1, 2, 0, 3)),
        jnp.transpose(hardening[0], (1, 0, 2)), jnp.transpose(ply_modulus[0], (1, 0, 2)),
        inverse_size, cost_map, migration_plan.reshape(cost_map.shape), block_nodes, corner_slot,
    )
    results = (disp, vel, moved, hardened)
    disp, vel, moved, hardened = pl.pallas_call(
        hand_over,
        out_shape=tuple(pltpu.HBM(x.shape, f32) for x in results),
        in_specs=[pl.BlockSpec(memory_space=pl.ANY)] * 4,
        out_specs=(every,) * 4,
        scratch_shapes=[dma((3 + kinds,))],
        compiler_params=pltpu.CompilerParams(vmem_limit_bytes=1024 * 1024),
    )(*results)
    return (
        disp.reshape(displacement.shape),
        vel.reshape(displacement.shape),
        jnp.transpose(moved, (2, 0, 1, 3))[None],
        jnp.transpose(hardened, (1, 0, 2))[None],
    )


def solution(mesh):
    return jax.shard_map(
        on_device,
        mesh=mesh,
        in_specs=(
            P("span", None, "grp"),
            P("span", None, "grp"),
            P("span", None, "grp"),
            P("span", "grp"),
            P("span", "grp", None, None, None),
            P("span", "grp", None, None),
            P("span", "grp", None, None),
            P("span", "grp", None),
            P("span", None),
            P("span", None, None),
            P("span", None, None),
            P("span", None, None, None),
        ),
        out_specs=(
            P("span", None, "grp"),
            P("span", None, "grp"),
            P("span", "grp", None, None, None),
            P("span", "grp", None, None),
        ),
        check_vma=False,
    )
```
